32 devices in a mesh: skyx: 4 (over y, core), skyy: 8 (over z, x).
Axes of the slice: x: 2, y: 2, z: 4, core: 2. Of those that a mesh axis runs over, the one named last changes fastest.
Arguments:
- image: bfloat16 [512, 16, 512], P(('skyx', 'skyy')), may hold values from -6 to 6
- inverse_var: bfloat16 [512, 16, 512], P(('skyx', 'skyy')), may hold values from 0.099609375 to 1
- patch_of: int32 [512, 1], replicated, may hold values from 0 to 31; in each aligned block of 16 rows (0 to 15, 16 to 31, ...) no two rows name the same one
- row_of: int32 [512], replicated, may hold values from 0 to 3
- valid: int32 [512], replicated, may hold values 0 or 1
- coef_index: int32 [32], replicated, may hold values from 0 to 63
- coef_table: float32 [64, 20], replicated, may hold values from -1.25 to 1.25
- basis_across: float32 [20, 41], replicated, may hold values from -1 to 1
- basis_down: float32 [20, 41], replicated, may hold values from -1 to 1
Outputs:
- coadd: float32 [512, 2048], P('skyy', 'skyx')
- weight_sum: float32 [512, 2048], P('skyy', 'skyx')
The draws below stay inside these ranges and needn't reach their ends.
Inputs may be any that keep to these rules, and one draw needn't show every extreme that they name: `patch_of`: within the 16 blocks of one exposure (the rows of one device) no patch appears twice.
All inputs are finite; a program needn't handle non-finite values.
Results may differ from the reference program's by a relative error of at most 0.0065.
Values may be sent and summed in bfloat16 or wider, within the bound.
A program may use at most 192 MiB of HBM per device.

```python
import math
import jax
import jax.numpy as jnp
import numpy as np
from jax import lax

BW = 512
BR = 16
RS = 4
NCHAN = 20
TAPS = 41
NCOEF = 64
OUTW = 640
PR = 64
EXPOSURES = 32
NB = 16
BLOCKS = 512
N_SKYX = 4
N_SKYY = 8


def plant(drawn, stream_key, smallest, largest):
    longest = drawn.shape.index(max(drawn.shape))
    spots = []
    for shift in (0, 1):
        where = [jax.random.randint(jax.random.fold_in(stream_key, axis), (), 0, length) for axis, length in enumerate(drawn.shape)]
        where[longest] = (where[longest] + shift) % drawn.shape[longest]
        spots.append(tuple(where))
    return drawn.at[spots[0]].set(smallest).at[spots[1]].set(largest)


def levels(own_key, shape, pieces, least, top_value):
    def one(dim, blocks):
        steps = jax.random.uniform(jax.random.fold_in(jax.random.fold_in(own_key, 6), dim), (blocks,), jnp.float32, least / len(pieces), top_value / len(pieces))
        return jnp.repeat(jnp.exp(steps), shape[dim] // blocks).reshape((-1,) + (1,) * (len(shape) - dim - 1))

    loudness = one(*pieces[0])
    for cut in pieces[1:]:
        loudness = loudness * one(*cut)
    return loudness


def routed_block(rng, own, number, rows, number_of, top, limit, lean):
    sequence = jax.random.permutation(rng, number_of)
    heavy_load, ordinary = portions_of(number_of, rows * top, limit, lean, True), portions_of(number_of, rows * top, limit, lean, False)
    places = jnp.arange(number_of)

    def named(sizes, offset_by):
        used = int((sizes > 0).sum())
        fixed = max(1, used // 4)
        moved = fixed + (places - fixed + offset_by * (used - fixed)) % max(1, number_of - fixed)
        return jnp.zeros((number_of,), jnp.int32).at[sequence[jnp.where(places < fixed, places, moved)]].set(jnp.asarray(sizes, jnp.int32))

    sizes = jnp.where(number % 4 == 0, named(heavy_load, number // 4), named(ordinary, number - number // 4 - 1))
    mixed = jax.random.permutation(jax.random.fold_in(own, 3), number_of)
    donor, sink = mixed[0:number_of // 2 * 2:2], mixed[1:number_of // 2 * 2:2]
    room = jnp.minimum(sizes[donor] - 1, limit - sizes[sink]) // 2
    room = jnp.where((donor == sequence[0]) | (sink == sequence[0]) | (sizes[sink] == 0), 0, jnp.maximum(room, 0))
    moved = jax.random.randint(jax.random.fold_in(own, 4), (number_of // 2,), 0, 1 << 20) % (room + 1)
    sizes = sizes.at[donor].add(-moved).at[sink].add(moved)
    items = jnp.searchsorted(jnp.cumsum(sizes), jnp.arange(rows * top), side="right").astype(jnp.int32)
    grid = items.reshape(top, rows).T
    grid = grid[jax.random.permutation(jax.random.fold_in(own, 1), rows)]
    offset_by = jax.random.randint(jax.random.fold_in(own, 2), (rows, 1), 0, top)
    return jnp.take_along_axis(grid, (jnp.arange(top)[None, :] + offset_by) % top, axis=1)


def portions_of(number_of, total, most, slope, full):
    weights = [(1 << 20) // math.isqrt(rank ** slope) + 1 for rank in range(1, number_of + 1)]
    largest = most if full else min(most, max(-(-total // number_of), total * weights[0] // sum(weights)))
    least = 1 if total - largest >= number_of - 1 else 0
    counts, spare = [largest] + [least] * (number_of - 1), total - largest - least * (number_of - 1)
    while spare > 0:
        candidates = [i for i in range(1, number_of) if counts[i] < largest] or [i for i in range(1, number_of) if counts[i] < most]
        mass, remaining = sum([weights[i] for i in candidates]), spare
        for i in candidates:
            more = min(most - counts[i], max(1, remaining * weights[i] // mass), spare)
            counts[i] = counts[i] + more
            spare = spare - more
    return np.array(counts)


def gaussian(stream_key, extent, spread, limit, split=(), kind=jnp.bfloat16):
    drawn = spread * jax.random.normal(stream_key, extent, jnp.float32)
    if split:
        drawn = drawn * levels(stream_key, extent, split, -0.22, 0.18)
    return jnp.clip(drawn, -limit, limit).astype(kind)


def setup_inputs(seed: int = 0) -> dict:
    key_list = jax.random.split(jax.random.key(seed), 10)
    image = gaussian(key_list[0], (BLOCKS, BR, BW), 1.0, 6.0, ((0, 32),))
    inverse_var = jnp.clip(jnp.exp(math.log(1.0) - 2.306499 * jax.random.uniform(key_list[1], (BLOCKS, BR, BW), jnp.float32) ** levels(key_list[1], (BLOCKS, BR, BW), ((0, 32),), -0.2, 0.2)), 0.099609375, 1.0).astype(jnp.bfloat16)
    patch_of_keys = jax.random.split(jax.random.fold_in(key_list[2], 1), BLOCKS // NB)
    patch_of_turns = jax.random.permutation(jax.random.fold_in(key_list[2], 3), BLOCKS // NB)
    patch_of = jax.vmap(lambda own, number: routed_block(jax.random.fold_in(key_list[2], 2), own, number, NB, EXPOSURES, 1, 1, 2))(patch_of_keys, patch_of_turns).reshape((BLOCKS, 1))
    row_of = plant(jax.random.randint(key_list[3], (BLOCKS,), 0, RS), jax.random.fold_in(key_list[3], 1), 0, RS - 1).astype(jnp.int32)
    valid = plant((jax.random.randint(key_list[4], (BLOCKS,), 0, 8) < 7).astype(jnp.int32), jax.random.fold_in(key_list[4], 1), 0, 1)
    coef_index = plant(jax.random.randint(key_list[5], (EXPOSURES,), 0, NCOEF), jax.random.fold_in(key_list[5], 1), 0, NCOEF - 1).astype(jnp.int32)
    coef_table = gaussian(key_list[6], (NCOEF, NCHAN), NCHAN ** -0.5, 1.25, (), jnp.float32)
    basis_across = gaussian(key_list[7], (NCHAN, TAPS), TAPS ** -0.5, 1.0, (), jnp.float32)
    basis_down = gaussian(key_list[8], (NCHAN, TAPS), TAPS ** -0.5, 1.0, (), jnp.float32)
    return {"image": image, "inverse_var": inverse_var, "patch_of": patch_of, "row_of": row_of, "valid": valid, "coef_index": coef_index, "coef_table": coef_table, "basis_across": basis_across, "basis_down": basis_down}


def across_matrix(basis_across):
    margin = (basis_across.shape[1] - 1) // 2
    rows_in = jnp.arange(128 + 2 * margin, dtype=jnp.int32)[:, None]
    cols_out = jnp.arange(128, dtype=jnp.int32)[None, :]
    offset = cols_out + 2 * margin - rows_in
    inside = (offset >= 0) & (offset <= 2 * margin)
    picked = jnp.take(basis_across, jnp.clip(offset, 0, 2 * margin), axis=1)
    return jnp.where(inside[None], picked, 0.0).astype(jnp.bfloat16)


def vertical_mix(basis_down, coeffs, row_count):
    margin = (basis_down.shape[1] - 1) // 2
    rows_out = jnp.arange(row_count + 2 * margin, dtype=jnp.int32)[:, None]
    rows_in = jnp.arange(row_count, dtype=jnp.int32)[None, :]
    offset = rows_out - rows_in
    inside = (offset >= 0) & (offset <= 2 * margin)
    picked = jnp.where(inside[None], jnp.take(basis_down, jnp.clip(offset, 0, 2 * margin), axis=1), 0.0)
    mixed_taps = coeffs[:, :, None, None] * picked[None]
    mixed_taps = jnp.transpose(mixed_taps, (0, 2, 1, 3))
    return mixed_taps.reshape(mixed_taps.shape[0], row_count + 2 * margin, -1).astype(jnp.bfloat16)


def convolve(planes, coeffs, across, basis_down, out_width):
    block_count, row_count, block_width = planes.shape
    margin = (basis_down.shape[1] - 1) // 2
    padded = jnp.pad(planes, ((0, 0), (0, 0), (2 * margin, out_width - block_width)))
    column_tiles = jnp.stack([padded[:, :, 128 * tile_index:128 * tile_index + 128 + 2 * margin] for tile_index in range(out_width // 128)], axis=1)
    swept_rows = jnp.einsum("ktri,cio->kcrto", column_tiles.astype(jnp.float32), across.astype(jnp.float32)).astype(jnp.bfloat16)
    swept_rows = swept_rows.reshape(block_count, -1, out_width)
    mixer_taps = vertical_mix(basis_down, coeffs, row_count)
    return jnp.einsum("kyj,kjx->kyx", mixer_taps.astype(jnp.float32), swept_rows.astype(jnp.float32)).astype(jnp.bfloat16)


def reference(image, inverse_var, patch_of, row_of, valid, coef_index, coef_table, basis_across, basis_down):
    margin = (TAPS - 1) // 2
    valid_flags = valid.astype(jnp.float32)[:, None, None]
    kept_planes = (valid_flags * inverse_var.astype(jnp.float32)).astype(jnp.bfloat16)
    weighted = (valid_flags * inverse_var.astype(jnp.float32) * image.astype(jnp.float32)).astype(jnp.bfloat16)
    choose = (coef_index[:, None] == jnp.arange(NCOEF, dtype=jnp.int32)[None, :]).astype(jnp.float32)
    coeffs = jnp.dot(choose, coef_table, precision=lax.Precision.HIGHEST)
    patch_ids = patch_of[:, 0]
    top_rows = ((patch_ids % N_SKYY) * PR + row_of * BR).astype(jnp.int32)
    left_cols = ((patch_ids // N_SKYY) * BW).astype(jnp.int32)
    across = across_matrix(basis_across)
    flux_sum = jnp.zeros((N_SKYY * PR + 2 * margin, N_SKYX * BW - BW + OUTW), jnp.float32)
    weight = jnp.zeros((N_SKYY * PR, N_SKYX * BW), jnp.float32)

    def per_exposure(state_in, inputs):
        planes, kept_rows, coef_row, tops_here, lefts_here = inputs
        rows_coef = jnp.broadcast_to(coef_row[None, :], (planes.shape[0], coef_row.shape[0]))
        contrib = convolve(planes, rows_coef, across, basis_down, OUTW)

        def place_one(position, state):
            flux_now, weight_now = state
            top_row = tops_here[position]
            left_col = lefts_here[position]
            window = lax.dynamic_slice(flux_now, (top_row, left_col), (contrib.shape[1], contrib.shape[2]))
            flux_now = lax.dynamic_update_slice(flux_now, window + contrib[position].astype(jnp.float32), (top_row, left_col))
            window = lax.dynamic_slice(weight_now, (top_row, left_col), (kept_rows.shape[1], kept_rows.shape[2]))
            weight_now = lax.dynamic_update_slice(weight_now, window + kept_rows[position].astype(jnp.float32), (top_row, left_col))
            return flux_now, weight_now

        return lax.fori_loop(0, planes.shape[0], place_one, state_in), None

    inputs = (weighted.reshape(EXPOSURES, NB, BR, BW), kept_planes.reshape(EXPOSURES, NB, BR, BW), coeffs,
              top_rows.reshape(EXPOSURES, NB), left_cols.reshape(EXPOSURES, NB))
    (flux_sum, weight), _ = lax.scan(per_exposure, (flux_sum, weight), inputs)
    return flux_sum[margin:margin + N_SKYY * PR, margin:margin + N_SKYX * BW], weight
```

```python
import functools

import jax
import jax.numpy as jnp
from jax import lax
from jax.experimental import pallas as pl
from jax.experimental.pallas import tpu as pltpu
from jax.sharding import PartitionSpec as P

RS = 4
LANES = 128
LEAD = 4
GROUP = 4
MESH = pl.DeviceIdType.MESH


def kernel(
    nx,
    ny,
    taps,
    pick_ref,
    image_ref,
    ivar_ref,
    code_ref,
    coef_ref,
    table_ref,
    across_ref,
    down_ref,
    coadd_ref,
    weight_ref,
    send,
    recv,
    across_pad,
    down_pad,
    coef_rows,
    chosen,
    bands,
    mixer,
    total,
    ext,
    edge_rows,
    edge_cols,
    edge_corners,
    send_sem,
    recv_sem,
    edge_send_sem,
    edge_recv_sem,
):
    count = nx * ny
    _, rows, width = image_ref.shape
    patch_rows = RS * rows
    channels = across_ref.shape[0]
    margin = (taps - 1) // 2
    tall = ext.shape[0]
    tiles = width // LANES
    spill = margin + LEAD
    mx = lax.axis_index("skyx")
    my = lax.axis_index("skyy")
    me = mx * ny + my

    def partner(step):
        tx = lax.rem(mx + step // ny, nx)
        ty = lax.rem(my + lax.rem(step, ny), ny)
        return tx, ty

    barrier = pltpu.get_barrier_semaphore()

    def greet(step, carry):
        tx, ty = partner(step)
        pl.semaphore_signal(barrier, inc=1, device_id=(tx, ty), device_id_type=MESH)
        return carry

    lax.fori_loop(1, count, greet, 0)

    def stage(patch, carry):
        block = pick_ref[patch]
        weight = ivar_ref[block].astype(jnp.float32)
        send[0, patch] = (weight * image_ref[block].astype(jnp.float32)).astype(jnp.bfloat16)
        send[1, patch] = ivar_ref[block]
        return carry

    lax.fori_loop(0, count, stage, 0)
    recv[0, me] = send[0, me]
    recv[1, me] = send[1, me]
    pl.semaphore_wait(barrier, count - 1)

    def block_copy(plane, target, source, device):
        return pltpu.make_async_remote_copy(
            src_ref=send.at[plane, target],
            dst_ref=recv.at[plane, source],
            send_sem=send_sem.at[plane, target],
            recv_sem=recv_sem.at[plane, source],
            device_id=device,
            device_id_type=MESH,
        )

    for plane in range(2):

        def start(step, carry):
            tx, ty = partner(step)
            block_copy(plane, tx * ny + ty, me, (tx, ty)).start()
            return carry

        lax.fori_loop(1, count, start, 0)

    across_pad[...] = jnp.zeros_like(across_pad)
    across_pad[:, :taps] = across_ref[...]
    down_pad[...] = jnp.zeros_like(down_pad)
    down_pad[:, :taps] = down_ref[...]
    down_pad[...] = pltpu.roll(down_pad[...], LEAD, 1)
    code = code_ref[...]
    place = lax.broadcasted_iota(jnp.int32, (patch_rows, code.shape[1]), 0)
    chosen_rows = (place == code).astype(jnp.float32).astype(jnp.bfloat16)
    chosen[:patch_rows] = chosen_rows
    chosen[patch_rows:] = chosen_rows
    sets = lax.broadcasted_iota(jnp.int32, (table_ref.shape[0], code.shape[1]), 0)
    coef_rows[...] = lax.dot_general(
        table_ref[...],
        (sets == coef_ref[...]).astype(jnp.float32),
        (((0,), (0,)), ((), ())),
        precision=lax.Precision.HIGHEST,
        preferred_element_type=jnp.float32,
    )

    def build(channel, carry):
        row = jnp.broadcast_to(across_pad[pl.ds(channel, 1), :], (LANES, 2 * LANES))
        band = pltpu.roll(row, 0, 1, stride=1, stride_axis=0)
        bands[channel, :LANES] = band[:, LANES:].astype(jnp.bfloat16)
        bands[channel, LANES:] = band[:, :LANES].astype(jnp.bfloat16)
        row = jnp.broadcast_to(down_pad[pl.ds(channel, 1), :], (patch_rows, LANES))
        shifted = pltpu.roll(row, 0, 1, stride=1, stride_axis=0)
        high = shifted.astype(jnp.bfloat16)
        low = (shifted - high.astype(jnp.float32)).astype(jnp.bfloat16)
        picked = lax.dot_general(
            jnp.concatenate([high, low], axis=0),
            chosen[...],
            (((0,), (0,)), ((), ())),
            preferred_element_type=jnp.float32,
        )
        mixed = picked[:tall] * coef_rows[pl.ds(channel, 1), :]
        start_row = pl.multiple_of(channel * tall, 16)
        mixer[pl.ds(start_row, tall), :] = mixed.astype(jnp.bfloat16)
        return carry

    lax.fori_loop(0, channels, build, 0)
    total[...] = jnp.zeros_like(total)

    def arrive(plane):
        def wait(step, carry):
            tx, ty = partner(step)
            block_copy(plane, me, tx * ny + ty, (tx, ty)).wait_recv()
            return carry

        lax.fori_loop(1, count, wait, 0)

    arrive(0)
    planes = recv[0].reshape(count * rows, width)
    zeros = jnp.zeros((tall, LANES), jnp.bfloat16)

    def convolve(turn, carry):
        start_row = pl.multiple_of(turn * GROUP * tall, 16)
        mixed = jnp.dot(
            mixer[pl.ds(start_row, GROUP * tall), :], planes, preferred_element_type=jnp.float32
        ).astype(jnp.bfloat16)
        summed = total[...]
        for member in range(GROUP):
            own = mixed[member * tall : (member + 1) * tall]
            padded = jnp.concatenate([zeros, own, zeros], axis=1)
            pairs = jnp.concatenate(
                [padded[:, LANES * t : LANES * (t + 2)] for t in range(tiles + 1)], axis=0
            )
            summed = summed + jnp.dot(
                pairs, bands[turn * GROUP + member], preferred_element_type=jnp.float32
            )
        total[...] = summed
        return carry

    lax.fori_loop(0, channels // GROUP, convolve, 0)
    joined = jnp.concatenate([total[t * tall : (t + 1) * tall] for t in range(tiles + 1)], axis=1)
    ext[...] = pltpu.roll(joined, width + LANES - margin, 1)

    top, middle, bottom = pl.ds(0, spill), pl.ds(spill, patch_rows), pl.ds(spill + patch_rows, spill)
    side, body_cols = pl.ds(width, LANES), pl.ds(0, width)
    plan = [
        (0, -1, (top, body_cols), edge_rows.at[1]),
        (0, 1, (bottom, body_cols), edge_rows.at[0]),
        (-1, 0, (middle, side), edge_cols.at[1]),
        (1, 0, (middle, side), edge_cols.at[0]),
        (-1, -1, (top, side), edge_corners.at[3]),
        (1, -1, (top, side), edge_corners.at[2]),
        (-1, 1, (bottom, side), edge_corners.at[1]),
        (1, 1, (bottom, side), edge_corners.at[0]),
    ]

    def exists(dx, dy):
        return (mx + dx >= 0) & (mx + dx < nx) & (my + dy >= 0) & (my + dy < ny)

    def edge_copy(number):
        dx, dy, piece, landing = plan[number]
        return pltpu.make_async_remote_copy(
            src_ref=ext.at[piece],
            dst_ref=landing,
            send_sem=edge_send_sem.at[number],
            recv_sem=edge_recv_sem.at[number],
            device_id=(mx + dx, my + dy),
            device_id_type=MESH,
        )

    for number, (dx, dy, _, _) in enumerate(plan):

        @pl.when(exists(dx, dy))
        def _():
            edge_copy(number).start()

    coadd_ref[...] = ext[middle, body_cols]

    arrive(1)
    weight_ref[...] = jnp.dot(
        chosen_rows_of(chosen, patch_rows),
        recv[1].reshape(count * rows, width),
        preferred_element_type=jnp.float32,
    )

    lane = lax.broadcasted_iota(jnp.int32, (spill, LANES), 1)
    lane_tall = lax.broadcasted_iota(jnp.int32, (patch_rows, LANES), 1)
    low_rows, high_rows = pl.ds(0, spill), pl.ds(patch_rows - spill, spill)
    left, right = pl.ds(0, LANES), pl.ds(width - LANES, LANES)

    def from_side(value, lanes, dx):
        if dx < 0:
            return jnp.where(lanes < margin, value, 0.0)
        return jnp.where(lanes >= LANES - margin, value, 0.0)

    for number, (dx, dy, _, landing) in enumerate(plan):
        @pl.when(exists(-dx, -dy))
        def _():
            edge_copy(number).wait_recv()
            if dx == 0:
                here = low_rows if dy > 0 else high_rows
                coadd_ref[here, :] += landing[...]
            elif dy == 0:
                here = left if dx > 0 else right
                coadd_ref[:, here] += from_side(landing[...], lane_tall, -dx)
            else:
                here = (low_rows if dy > 0 else high_rows, left if dx > 0 else right)
                coadd_ref[here] += from_side(landing[...], lane, -dx)

    for plane in range(2):

        def sent(step, carry):
            tx, ty = partner(step)
            block_copy(plane, tx * ny + ty, me, (tx, ty)).wait_send()
            return carry

        lax.fori_loop(1, count, sent, 0)
    for number, (dx, dy, _, _) in enumerate(plan):

        @pl.when(exists(dx, dy))
        def _():
            edge_copy(number).wait_send()


def chosen_rows_of(chosen, patch_rows):
    return chosen[:patch_rows]


def body(
    image, inverse_var, patch_of, row_of, valid, coef_index, coef_table, basis_across, basis_down
):
    nx, ny = lax.axis_size("skyx"), lax.axis_size("skyy")
    count = nx * ny
    blocks, rows, width = image.shape
    channels, taps = basis_across.shape
    margin = (taps - 1) // 2
    patch_rows = RS * rows
    spill = margin + LEAD
    tall = patch_rows + 2 * spill
    tiles = width // LANES
    me = lax.axis_index("skyx") * ny + lax.axis_index("skyy")
    targets = patch_of[:, 0].reshape(count, blocks)
    mine = lax.dynamic_slice_in_dim(targets, me, 1)
    patches = jnp.arange(count, dtype=jnp.int32)[:, None]
    slots = jnp.arange(blocks, dtype=jnp.int32)[None, :]
    pick = jnp.sum(jnp.where(mine == patches, slots, 0), axis=1)
    usable = (targets == me) & (valid.reshape(count, blocks) > 0)
    far = 1 << 20
    first = jnp.sum(jnp.where(usable, row_of.reshape(count, blocks) * rows + far, 0), axis=1) - far
    code = (first[:, None] + jnp.arange(rows, dtype=jnp.int32)[None, :]).reshape(1, count * rows)
    sets = jnp.broadcast_to(coef_index[:, None], (count, rows)).reshape(1, count * rows)

    vmem = pl.BlockSpec(memory_space=pltpu.VMEM)
    smem = pl.BlockSpec(memory_space=pltpu.SMEM)
    deep = count * rows
    return pl.pallas_call(
        functools.partial(kernel, nx, ny, taps),
        out_shape=(
            jax.ShapeDtypeStruct((patch_rows, width), jnp.float32),
            jax.ShapeDtypeStruct((patch_rows, width), jnp.float32),
        ),
        in_specs=[smem] + [vmem] * 7,
        out_specs=(vmem, vmem),
        scratch_shapes=[
            pltpu.VMEM((2, count, rows, width), jnp.bfloat16),
            pltpu.VMEM((2, count, rows, width), jnp.bfloat16),
            pltpu.VMEM((channels, 2 * LANES), jnp.float32),
            pltpu.VMEM((channels, LANES), jnp.float32),
            pltpu.VMEM((channels, deep), jnp.float32),
            pltpu.VMEM((2 * patch_rows, deep), jnp.bfloat16),
            pltpu.VMEM((channels, 2 * LANES, LANES), jnp.bfloat16),
            pltpu.VMEM((channels * tall, deep), jnp.bfloat16),
            pltpu.VMEM(((tiles + 1) * tall, LANES), jnp.float32),
            pltpu.VMEM((tall, width + LANES), jnp.float32),
            pltpu.VMEM((2, spill, width), jnp.float32),
            pltpu.VMEM((2, patch_rows, LANES), jnp.float32),
            pltpu.VMEM((4, spill, LANES), jnp.float32),
            pltpu.SemaphoreType.DMA((2, count)),
            pltpu.SemaphoreType.DMA((2, count)),
            pltpu.SemaphoreType.DMA((8,)),
            pltpu.SemaphoreType.DMA((8,)),
        ],
        compiler_params=pltpu.CompilerParams(
            collective_id=0, has_side_effects=True, vmem_limit_bytes=48 * 1024 * 1024
        ),
    )(pick, image, inverse_var, code, sets, coef_table, basis_across, basis_down)


def solution(mesh):
    placed = (
        P(("skyx", "skyy"), None, None),
        P(("skyx", "skyy"), None, None),
        P(),
        P(),
        P(),
        P(),
        P(),
        P(),
        P(),
    )
    return jax.shard_map(
        body,
        mesh=mesh,
        in_specs=placed,
        out_specs=(P("skyy", "skyx"), P("skyy", "skyx")),
        check_vma=False,
    )
```

```python
import functools

import jax
import jax.numpy as jnp
from jax import lax
from jax.experimental import pallas as pl
from jax.experimental.pallas import tpu as pltpu
from jax.sharding import PartitionSpec as P

RS = 4
LANES = 128
LEAD = 4
INNER = 2
GROUP = 4
MESH = pl.DeviceIdType.MESH


def kernel(
    nx,
    ny,
    taps,
    image_hbm,
    ivar_hbm,
    patch_hbm,
    row_hbm,
    valid_hbm,
    sets_hbm,
    table_hbm,
    across_hbm,
    down_hbm,
    coadd_ref,
    weight_ref,
    image_ref,
    ivar_ref,
    patch_scalars,
    patch_lanes,
    row_lanes,
    valid_lanes,
    sets_lanes,
    table_ref,
    across_ref,
    down_ref,
    send,
    recv,
    keep_send,
    keep_recv,
    part_send,
    part_recv,
    across_pad,
    down_pad,
    coef_rows,
    chosen,
    bands,
    mixer,
    mixed_tiles,
    ext,
    edge_rows,
    edge_cols,
    edge_corners,
    load_sem,
    send_sem,
    recv_sem,
    keep_send_sem,
    keep_recv_sem,
    part_send_sem,
    part_recv_sem,
    edge_send_sem,
    edge_recv_sem,
):
    count = nx * ny
    planes = ny // INNER
    members = nx * INNER
    blocks, rows, width = image_ref.shape
    patch_rows = RS * rows
    channels = across_ref.shape[0]
    margin = (taps - 1) // 2
    tall = ext.shape[0]
    tiles = width // LANES
    spill = margin + LEAD
    mx = lax.axis_index("skyx")
    my = lax.axis_index("skyy")
    me = mx * ny + my
    hi, lo = my // INNER, lax.rem(my, INNER)

    def partner(step):
        back = count - 1 - step
        tx = lax.rem(mx + lax.rem(back // INNER, nx), nx)
        thi = lax.rem(hi + back // members, planes)
        tlo = lax.rem(lo + lax.rem(back, INNER), INNER)
        return tx, thi, tlo

    barrier = pltpu.get_barrier_semaphore()
    pairs = [
        (patch_hbm, patch_scalars),
        (image_hbm, image_ref),
        (ivar_hbm, ivar_ref),
        (patch_hbm, patch_lanes),
        (row_hbm, row_lanes),
        (valid_hbm, valid_lanes),
        (sets_hbm, sets_lanes),
        (table_hbm, table_ref),
        (across_hbm, across_ref),
        (down_hbm, down_ref),
    ]
    loads = [
        pltpu.make_async_copy(source, landing, load_sem.at[number])
        for number, (source, landing) in enumerate(pairs)
    ]
    for load in loads:
        load.start()

    def greet(step, carry):
        tx, thi, tlo = partner(step)
        pl.semaphore_signal(
            barrier, inc=1, device_id=(tx, thi * INNER + tlo), device_id_type=MESH
        )
        return carry

    lax.fori_loop(0, count - 1, greet, 0)
    for load in loads[:3]:
        load.wait()
    targets = [patch_scalars[0, me * blocks + k] for k in range(blocks)]

    def stage(tx, thi, tlo):
        patch = tx * ny + thi * INNER + tlo
        block = 0
        for k in range(1, blocks):
            block = jnp.where(targets[k] == patch, k, block)
        weight = ivar_ref[block]
        product = weight.astype(jnp.float32) * image_ref[block].astype(jnp.float32)
        send[patch] = product.astype(jnp.bfloat16)
        keep_send[tx * INNER + tlo, thi] = weight
        return patch

    def block_copy(target, source, device):
        return pltpu.make_async_remote_copy(
            src_ref=send.at[target],
            dst_ref=recv.at[source],
            send_sem=send_sem.at[target],
            recv_sem=recv_sem.at[source],
            device_id=device,
            device_id_type=MESH,
        )

    def keep_copy(target, source, device):
        return pltpu.make_async_remote_copy(
            src_ref=keep_send.at[target],
            dst_ref=keep_recv.at[source],
            send_sem=keep_send_sem.at[target],
            recv_sem=keep_recv_sem.at[source],
            device_id=device,
            device_id_type=MESH,
        )

    def part_copy(target, source, device):
        return pltpu.make_async_remote_copy(
            src_ref=part_send.at[target],
            dst_ref=part_recv.at[source],
            send_sem=part_send_sem.at[target],
            recv_sem=part_recv_sem.at[source],
            device_id=device,
            device_id_type=MESH,
        )

    pl.semaphore_wait(barrier, count - 1)

    def start(step, carry):
        tx, thi, tlo = partner(step)
        patch = stage(tx, thi, tlo)
        block_copy(patch, me, (tx, thi * INNER + tlo)).start()
        return carry

    lax.fori_loop(0, count - 1, start, 0)
    stage(mx, hi, lo)
    recv[me] = send[me]

    def member_of(step):
        return lax.rem(mx + step // INNER, nx), lax.rem(lo + lax.rem(step, INNER), INNER)

    own_member = mx * INNER + lo

    def start_keep(step, carry):
        tx, tlo = member_of(step)
        keep_copy(tx * INNER + tlo, own_member, (tx, hi * INNER + tlo)).start()
        return carry

    lax.fori_loop(1, members, start_keep, 0)
    keep_recv[own_member] = keep_send[own_member]
    for load in loads[3:]:
        load.wait()

    across_pad[...] = jnp.zeros_like(across_pad)
    across_pad[:, :taps] = across_ref[...]
    down_pad[...] = jnp.zeros_like(down_pad)
    down_pad[:, :taps] = down_ref[...]
    down_pad[...] = pltpu.roll(down_pad[...], LEAD, 1)

    def same(condition):
        return condition.astype(jnp.float32).astype(jnp.bfloat16)

    def iota(shape, dim):
        return lax.broadcasted_iota(jnp.int32, shape, dim)

    def spread(slots, groups):
        lanes = slots.shape[1]
        tall_flags = jnp.concatenate(
            [jnp.broadcast_to(slots[s : s + 1], (rows, lanes)) for s in range(groups * RS)], axis=0
        )
        shape = tall_flags.shape
        keep = lax.rem(iota(shape, 0), rows) == lax.rem(iota(shape, 1), rows)
        return jnp.where(keep, tall_flags, 0.0).astype(jnp.bfloat16)

    spot = jnp.where(valid_lanes[...] > 0, patch_lanes[...] * RS + row_lanes[...], -1)
    wide = count * blocks
    own_slots = same(iota((8, wide), 0) + me * RS == spot)
    own_slots = jnp.where(iota((8, wide), 0) < RS, own_slots, jnp.bfloat16(0))
    chunk = LANES // rows
    repeat = same(
        iota((chunk * blocks, LANES), 0) // blocks == iota((chunk * blocks, LANES), 1) // rows
    )
    own_flags = jnp.concatenate(
        [
            jnp.dot(
                own_slots[:, g * chunk * blocks : (g + 1) * chunk * blocks],
                repeat,
                preferred_element_type=jnp.float32,
            )
            for g in range(count // chunk)
        ],
        axis=1,
    )
    own_rows = spread(own_flags, 1)
    chosen[:patch_rows] = own_rows
    chosen[patch_rows:] = own_rows

    onehot = (iota((table_ref.shape[1], count), 0) == sets_lanes[...]).astype(jnp.float32)
    coeffs = jnp.dot(
        table_ref[...],
        onehot,
        precision=lax.Precision.HIGHEST,
        preferred_element_type=jnp.float32,
    )
    deep = count * rows
    coef_rows[...] = jnp.dot(
        coeffs,
        (iota((count, deep), 0) == iota((count, deep), 1) // rows).astype(jnp.float32),
        precision=lax.Precision.HIGHEST,
        preferred_element_type=jnp.float32,
    )

    shape = (planes * RS, wide)
    wanted = (mx * ny + (iota(shape, 0) // RS) * INNER + lo) * RS + lax.rem(iota(shape, 0), RS)
    shape = (wide, members * rows)
    member = iota(shape, 1) // rows
    exposure = (member // INNER) * ny + hi * INNER + lax.rem(member, INNER)
    plane_flags = jnp.dot(
        same(wanted == spot),
        same(iota(shape, 0) // blocks == exposure),
        preferred_element_type=jnp.float32,
    )
    plane_rows = spread(plane_flags, planes)

    def build(channel, carry):
        row = jnp.broadcast_to(across_pad[pl.ds(channel, 1), :], (LANES, 2 * LANES))
        band = pltpu.roll(row, 0, 1, stride=1, stride_axis=0)
        bands[pl.ds(pl.multiple_of(channel * LANES, LANES), LANES), :] = band.astype(jnp.bfloat16)
        row = jnp.broadcast_to(down_pad[pl.ds(channel, 1), :], (patch_rows, LANES))
        shifted = pltpu.roll(row, 0, 1, stride=1, stride_axis=0)
        high = shifted.astype(jnp.bfloat16)
        low = (shifted - high.astype(jnp.float32)).astype(jnp.bfloat16)
        picked = lax.dot_general(
            jnp.concatenate([high, low], axis=0),
            chosen[...],
            (((0,), (0,)), ((), ())),
            preferred_element_type=jnp.float32,
        )
        mixed = picked[:tall] * coef_rows[pl.ds(channel, 1), :]
        start_row = pl.multiple_of(channel * tall, 16)
        mixer[pl.ds(start_row, tall), :] = mixed.astype(jnp.bfloat16)
        return carry

    lax.fori_loop(0, channels, build, 0)

    def wait_keep(step, carry):
        tx, tlo = member_of(step)
        keep_copy(own_member, tx * INNER + tlo, (tx, hi * INNER + tlo)).wait_recv()
        return carry

    lax.fori_loop(1, members, wait_keep, 0)
    for plane in range(planes):
        part_send[plane] = jnp.dot(
            plane_rows[plane * patch_rows : (plane + 1) * patch_rows],
            keep_recv[:, plane].reshape(members * rows, width),
            preferred_element_type=jnp.float32,
        ).astype(jnp.bfloat16)
    part_recv[hi] = part_send[hi]

    def wait_block(step, carry):
        tx, thi, tlo = partner(step)
        ty = thi * INNER + tlo
        block_copy(me, tx * ny + ty, (tx, ty)).wait_recv()
        return carry

    lax.fori_loop(0, count - 1, wait_block, 0)

    def plane_at(step):
        return lax.rem(hi + step, planes)

    def start_part(step, carry):
        thi = plane_at(step)
        part_copy(thi, hi, (mx, thi * INNER + lo)).start()
        return carry

    lax.fori_loop(1, planes, start_part, 0)
    arrived = recv[...].reshape(deep, width)
    for turn in range(channels // GROUP):
        mixed = jnp.dot(
            mixer[turn * GROUP * tall : (turn + 1) * GROUP * tall],
            arrived,
            preferred_element_type=jnp.float32,
        ).astype(jnp.bfloat16)
        for member in range(GROUP):
            channel = turn * GROUP + member
            for t in range(tiles):
                mixed_tiles[
                    t * tall : (t + 1) * tall, channel * LANES : (channel + 1) * LANES
                ] = mixed[member * tall : (member + 1) * tall, t * LANES : (t + 1) * LANES]
    summed = jnp.dot(mixed_tiles[...], bands[...], preferred_element_type=jnp.float32)
    zeros = jnp.zeros((tall, LANES), jnp.float32)
    now = [summed[t * tall : (t + 1) * tall, :LANES] for t in range(tiles)] + [zeros]
    after = [zeros] + [summed[t * tall : (t + 1) * tall, LANES:] for t in range(tiles)]
    joined = jnp.concatenate([a + b for a, b in zip(now, after)], axis=1)
    ext[...] = pltpu.roll(joined, width + LANES - margin, 1)

    top, middle, bottom = pl.ds(0, spill), pl.ds(spill, patch_rows), pl.ds(spill + patch_rows, spill)
    side, body_cols = pl.ds(width, LANES), pl.ds(0, width)
    plan = [
        (0, -1, (top, body_cols), edge_rows.at[1]),
        (0, 1, (bottom, body_cols), edge_rows.at[0]),
        (-1, 0, (middle, side), edge_cols.at[1]),
        (1, 0, (middle, side), edge_cols.at[0]),
        (-1, -1, (top, side), edge_corners.at[3]),
        (1, -1, (top, side), edge_corners.at[2]),
        (-1, 1, (bottom, side), edge_corners.at[1]),
        (1, 1, (bottom, side), edge_corners.at[0]),
    ]

    def exists(dx, dy):
        return (mx + dx >= 0) & (mx + dx < nx) & (my + dy >= 0) & (my + dy < ny)

    def edge_copy(number):
        dx, dy, piece, landing = plan[number]
        return pltpu.make_async_remote_copy(
            src_ref=ext.at[piece],
            dst_ref=landing,
            send_sem=edge_send_sem.at[number],
            recv_sem=edge_recv_sem.at[number],
            device_id=(mx + dx, my + dy),
            device_id_type=MESH,
        )

    for number, (dx, dy, _, _) in enumerate(plan):

        @pl.when(exists(dx, dy))
        def _():
            edge_copy(number).start()

    coadd_ref[...] = ext[middle, body_cols]

    def wait_part(step, carry):
        thi = plane_at(step)
        part_copy(hi, thi, (mx, thi * INNER + lo)).wait_recv()
        return carry

    lax.fori_loop(1, planes, wait_part, 0)
    weights = part_recv[0].astype(jnp.float32)
    for plane in range(1, planes):
        weights = weights + part_recv[plane].astype(jnp.float32)
    weight_ref[...] = weights

    lane = lax.broadcasted_iota(jnp.int32, (spill, LANES), 1)
    lane_tall = lax.broadcasted_iota(jnp.int32, (patch_rows, LANES), 1)
    low_rows, high_rows = pl.ds(0, spill), pl.ds(patch_rows - spill, spill)
    left, right = pl.ds(0, LANES), pl.ds(width - LANES, LANES)

    def from_side(value, lanes, dx):
        if dx < 0:
            return jnp.where(lanes < margin, value, 0.0)
        return jnp.where(lanes >= LANES - margin, value, 0.0)

    for number, (dx, dy, _, landing) in enumerate(plan):
        @pl.when(exists(-dx, -dy))
        def _():
            edge_copy(number).wait_recv()
            if dx == 0:
                here = low_rows if dy > 0 else high_rows
                coadd_ref[here, :] += landing[...]
            elif dy == 0:
                here = left if dx > 0 else right
                coadd_ref[:, here] += from_side(landing[...], lane_tall, -dx)
            else:
                here = (low_rows if dy > 0 else high_rows, left if dx > 0 else right)
                coadd_ref[here] += from_side(landing[...], lane, -dx)

    def sent_block(step, carry):
        tx, thi, tlo = partner(step)
        ty = thi * INNER + tlo
        block_copy(tx * ny + ty, me, (tx, ty)).wait_send()
        return carry

    def sent_keep(step, carry):
        tx, tlo = member_of(step)
        keep_copy(tx * INNER + tlo, own_member, (tx, hi * INNER + tlo)).wait_send()
        return carry

    def sent_part(step, carry):
        thi = plane_at(step)
        part_copy(thi, hi, (mx, thi * INNER + lo)).wait_send()
        return carry

    lax.fori_loop(0, count - 1, sent_block, 0)
    lax.fori_loop(1, members, sent_keep, 0)
    lax.fori_loop(1, planes, sent_part, 0)
    for number, (dx, dy, _, _) in enumerate(plan):

        @pl.when(exists(dx, dy))
        def _():
            edge_copy(number).wait_send()


def body(
    image, inverse_var, patch_of, row_of, valid, coef_index, coef_table, basis_across, basis_down
):
    nx, ny = lax.axis_size("skyx"), lax.axis_size("skyy")
    count = nx * ny
    planes, members = ny // INNER, nx * INNER
    blocks, rows, width = image.shape
    channels, taps = basis_across.shape
    margin = (taps - 1) // 2
    patch_rows = RS * rows
    spill = margin + LEAD
    tall = patch_rows + 2 * spill
    tiles = width // LANES
    deep = count * rows
    wide = count * blocks

    vmem = pl.BlockSpec(memory_space=pltpu.VMEM)
    anywhere = pl.BlockSpec(memory_space=pl.ANY)
    dma = pltpu.SemaphoreType.DMA
    return pl.pallas_call(
        functools.partial(kernel, nx, ny, taps),
        out_shape=(
            jax.ShapeDtypeStruct((patch_rows, width), jnp.float32),
            jax.ShapeDtypeStruct((patch_rows, width), jnp.float32),
        ),
        in_specs=[anywhere] * 9,
        out_specs=(vmem, vmem),
        scratch_shapes=[
            pltpu.VMEM((blocks, rows, width), jnp.bfloat16),
            pltpu.VMEM((blocks, rows, width), jnp.bfloat16),
            pltpu.SMEM((1, wide), jnp.int32),
            pltpu.VMEM((1, wide), jnp.int32),
            pltpu.VMEM((1, wide), jnp.int32),
            pltpu.VMEM((1, wide), jnp.int32),
            pltpu.VMEM((1, count), jnp.int32),
            pltpu.VMEM(coef_table.shape[::-1], jnp.float32),
            pltpu.VMEM((channels, taps), jnp.float32),
            pltpu.VMEM((channels, taps), jnp.float32),
            pltpu.VMEM((count, rows, width), jnp.bfloat16),
            pltpu.VMEM((count, rows, width), jnp.bfloat16),
            pltpu.VMEM((members, planes, rows, width), jnp.bfloat16),
            pltpu.VMEM((members, planes, rows, width), jnp.bfloat16),
            pltpu.VMEM((planes, patch_rows, width), jnp.bfloat16),
            pltpu.VMEM((planes, patch_rows, width), jnp.bfloat16),
            pltpu.VMEM((channels, 2 * LANES), jnp.float32),
            pltpu.VMEM((channels, LANES), jnp.float32),
            pltpu.VMEM((channels, deep), jnp.float32),
            pltpu.VMEM((2 * patch_rows, deep), jnp.bfloat16),
            pltpu.VMEM((channels * LANES, 2 * LANES), jnp.bfloat16),
            pltpu.VMEM((channels * tall, deep), jnp.bfloat16),
            pltpu.VMEM((tiles * tall, channels * LANES), jnp.bfloat16),
            pltpu.VMEM((tall, width + LANES), jnp.float32),
            pltpu.VMEM((2, spill, width), jnp.float32),
            pltpu.VMEM((2, patch_rows, LANES), jnp.float32),
            pltpu.VMEM((4, spill, LANES), jnp.float32),
            dma((10,)),
            dma((count,)),
            dma((count,)),
            dma((members,)),
            dma((members,)),
            dma((planes,)),
            dma((planes,)),
            dma((8,)),
            dma((8,)),
        ],
        compiler_params=pltpu.CompilerParams(
            collective_id=0, has_side_effects=True, vmem_limit_bytes=60 * 1024 * 1024
        ),
    )(
        image,
        inverse_var,
        patch_of.reshape(1, wide),
        row_of.reshape(1, wide),
        valid.reshape(1, wide),
        coef_index.reshape(1, count),
        coef_table.T,
        basis_across,
        basis_down,
    )


def solution(mesh):
    placed = (
        P(("skyx", "skyy"), None, None),
        P(("skyx", "skyy"), None, None),
        P(),
        P(),
        P(),
        P(),
        P(),
        P(),
        P(),
    )
    return jax.shard_map(
        body,
        mesh=mesh,
        in_specs=placed,
        out_specs=(P("skyy", "skyx"), P("skyy", "skyx")),
        check_vma=False,
    )
```

```python
import functools

import jax
import jax.numpy as jnp
from jax import lax
from jax.experimental import pallas as pl
from jax.experimental.pallas import tpu as pltpu
from jax.sharding import PartitionSpec as P

RS = 4
LANES = 128
LEAD = 4
INNER = 2
GROUP = 4
MESH = pl.DeviceIdType.MESH


def kernel(
    nx,
    ny,
    taps,
    image_hbm,
    ivar_hbm,
    patch_hbm,
    row_hbm,
    valid_hbm,
    sets_hbm,
    table_hbm,
    across_hbm,
    down_hbm,
    coadd_ref,
    weight_ref,
    image_ref,
    ivar_ref,
    patch_scalars,
    patch_lanes,
    row_lanes,
    valid_lanes,
    sets_lanes,
    table_ref,
    across_ref,
    down_ref,
    send,
    recv,
    keep_send,
    keep_recv,
    part_send,
    part_recv,
    across_pad,
    down_pad,
    coef_rows,
    chosen,
    bands,
    shifts,
    mixer,
    mixed_tiles,
    ext,
    edge_rows,
    edge_cols,
    edge_corners,
    load_sem,
    send_sem,
    recv_sem,
    keep_send_sem,
    keep_recv_sem,
    part_send_sem,
    part_recv_sem,
    edge_send_sem,
    edge_recv_sem,
):
    count = nx * ny
    planes = ny // INNER
    members = nx * INNER
    blocks, rows, width = image_ref.shape
    patch_rows = RS * rows
    channels = across_ref.shape[0]
    margin = (taps - 1) // 2
    tall = ext.shape[0]
    tiles = width // LANES
    spill = margin + LEAD
    mx = lax.axis_index("skyx")
    my = lax.axis_index("skyy")
    me = mx * ny + my
    hi, lo = my // INNER, lax.rem(my, INNER)

    def partner(step):
        back = count - 1 - step
        tx = lax.rem(mx + lax.rem(back // INNER, nx), nx)
        thi = lax.rem(hi + back // members, planes)
        tlo = lax.rem(lo + lax.rem(back, INNER), INNER)
        return tx, thi, tlo

    barrier = pltpu.get_barrier_semaphore()
    pairs = [
        (patch_hbm, patch_scalars),
        (image_hbm, image_ref),
        (ivar_hbm, ivar_ref),
        (patch_hbm, patch_lanes),
        (row_hbm, row_lanes),
        (valid_hbm, valid_lanes),
        (sets_hbm, sets_lanes),
        (table_hbm, table_ref),
        (across_hbm, across_ref),
        (down_hbm, down_ref),
    ]
    loads = [
        pltpu.make_async_copy(source, landing, load_sem.at[number])
        for number, (source, landing) in enumerate(pairs)
    ]
    for load in loads:
        load.start()

    def greet(step, carry):
        tx, thi, tlo = partner(step)
        pl.semaphore_signal(
            barrier, inc=1, device_id=(tx, thi * INNER + tlo), device_id_type=MESH
        )
        return carry

    lax.fori_loop(0, count - 1, greet, 0)
    for load in loads[:3]:
        load.wait()
    targets = [patch_scalars[0, me * blocks + k] for k in range(blocks)]

    def stage(tx, thi, tlo):
        patch = tx * ny + thi * INNER + tlo
        block = 0
        for k in range(1, blocks):
            block = jnp.where(targets[k] == patch, k, block)
        weight = ivar_ref[block]
        product = weight.astype(jnp.float32) * image_ref[block].astype(jnp.float32)
        send[patch] = product.astype(jnp.bfloat16)
        keep_send[tx * INNER + tlo, thi] = weight

    def block_copy(target, source, device):
        return pltpu.make_async_remote_copy(
            src_ref=send.at[target],
            dst_ref=recv.at[source],
            send_sem=send_sem.at[target],
            recv_sem=recv_sem.at[source],
            device_id=device,
            device_id_type=MESH,
        )

    def keep_copy(target, source, device):
        return pltpu.make_async_remote_copy(
            src_ref=keep_send.at[target],
            dst_ref=keep_recv.at[source],
            send_sem=keep_send_sem.at[target],
            recv_sem=keep_recv_sem.at[source],
            device_id=device,
            device_id_type=MESH,
        )

    def part_copy(target, source, device):
        return pltpu.make_async_remote_copy(
            src_ref=part_send.at[target],
            dst_ref=part_recv.at[source],
            send_sem=part_send_sem.at[target],
            recv_sem=part_recv_sem.at[source],
            device_id=device,
            device_id_type=MESH,
        )

    def prepare(step, carry):
        stage(*partner(step))
        return carry

    lax.fori_loop(0, count, prepare, 0)
    pl.semaphore_wait(barrier, count - 1)

    def start(step, carry):
        tx, thi, tlo = partner(step)
        ty = thi * INNER + tlo
        block_copy(tx * ny + ty, me, (tx, ty)).start()
        return carry

    lax.fori_loop(0, count - 1, start, 0)
    recv[me] = send[me]

    def member_of(step):
        return lax.rem(mx + step // INNER, nx), lax.rem(lo + lax.rem(step, INNER), INNER)

    own_member = mx * INNER + lo

    def start_keep(step, carry):
        tx, tlo = member_of(step)
        keep_copy(tx * INNER + tlo, own_member, (tx, hi * INNER + tlo)).start()
        return carry

    lax.fori_loop(1, members, start_keep, 0)
    keep_recv[own_member] = keep_send[own_member]
    for load in loads[3:]:
        load.wait()

    def same(condition):
        return condition.astype(jnp.float32).astype(jnp.bfloat16)

    def iota(shape, dim):
        return lax.broadcasted_iota(jnp.int32, shape, dim)

    def over(value, by):
        return value >> (by.bit_length() - 1) if by & (by - 1) == 0 else value // by

    def within(value, by):
        return value & (by - 1) if by & (by - 1) == 0 else lax.rem(value, by)

    def spread(slots, groups):
        lanes = slots.shape[1]
        tall_flags = jnp.concatenate(
            [jnp.broadcast_to(slots[s : s + 1], (rows, lanes)) for s in range(groups * RS)], axis=0
        )
        shape = tall_flags.shape
        keep = within(iota(shape, 0), rows) == within(iota(shape, 1), rows)
        return jnp.where(keep, tall_flags, 0.0).astype(jnp.bfloat16)

    spot = jnp.where(valid_lanes[...] > 0, patch_lanes[...] * RS + row_lanes[...], -1)
    wide = count * blocks
    own_slots = same(iota((8, wide), 0) + me * RS == spot)
    own_slots = jnp.where(iota((8, wide), 0) < RS, own_slots, jnp.bfloat16(0))
    chunk = LANES // rows
    repeat = same(
        over(iota((chunk * blocks, LANES), 0), blocks) == over(iota((chunk * blocks, LANES), 1), rows)
    )
    own_flags = jnp.concatenate(
        [
            jnp.dot(
                own_slots[:, g * chunk * blocks : (g + 1) * chunk * blocks],
                repeat,
                preferred_element_type=jnp.float32,
            )
            for g in range(count // chunk)
        ],
        axis=1,
    )
    own_rows = spread(own_flags, 1)
    chosen[:patch_rows] = own_rows
    chosen[patch_rows:] = own_rows

    onehot = (iota((table_ref.shape[1], count), 0) == sets_lanes[...]).astype(jnp.float32)
    coeffs = jnp.dot(
        table_ref[...],
        onehot,
        precision=lax.Precision.HIGHEST,
        preferred_element_type=jnp.float32,
    )
    deep = count * rows
    coef_rows[...] = jnp.dot(
        coeffs,
        (iota((count, deep), 0) == over(iota((count, deep), 1), rows)).astype(jnp.float32),
        precision=lax.Precision.HIGHEST,
        preferred_element_type=jnp.float32,
    )

    shape = (planes * RS, wide)
    wanted = (mx * ny + over(iota(shape, 0), RS) * INNER + lo) * RS + within(iota(shape, 0), RS)
    shape = (wide, members * rows)
    member = over(iota(shape, 1), rows)
    exposure = over(member, INNER) * ny + hi * INNER + within(member, INNER)
    plane_flags = jnp.dot(
        same(wanted == spot),
        same(over(iota(shape, 0), blocks) == exposure),
        preferred_element_type=jnp.float32,
    )
    plane_rows = spread(plane_flags, planes)

    tap = iota((taps, LANES), 0)
    lane = iota((taps, LANES), 1)

    def laid(filters, where_to):
        return jnp.dot(
            filters,
            (lane == where_to).astype(jnp.float32),
            precision=lax.Precision.HIGHEST,
            preferred_element_type=jnp.float32,
        )

    across_pad[...] = laid(across_ref[...], tap)
    down_pad[...] = laid(down_ref[...], LANES - LEAD - tap)
    forward = iota((LANES, LANES), 1) >= iota((LANES, LANES), 0)
    first_half = iota((tall, LANES), 1) < patch_rows

    def build_bands(channel, carry):
        row = jnp.broadcast_to(across_pad[pl.ds(channel, 1), :], (LANES, LANES))
        band = pltpu.roll(row, 0, 1, stride=1, stride_axis=0)
        start_row = pl.multiple_of(channel * LANES, LANES)
        bands[pl.ds(start_row, LANES), :LANES] = jnp.where(forward, band, 0.0).astype(jnp.bfloat16)
        bands[pl.ds(start_row, LANES), LANES:] = jnp.where(forward, 0.0, band).astype(jnp.bfloat16)
        row = jnp.broadcast_to(down_pad[pl.ds(channel, 1), :], (tall, LANES))
        shifted = pltpu.roll(row, 0, 1, stride=1, stride_axis=0)
        high = shifted.astype(jnp.bfloat16).astype(jnp.float32)
        low = pltpu.roll(shifted - high, patch_rows, 1)
        start_row = pl.multiple_of(channel * tall, 16)
        shifts[pl.ds(start_row, tall), :] = jnp.where(first_half, high, low).astype(jnp.bfloat16)
        return carry

    lax.fori_loop(0, channels, build_bands, 0, unroll=4)

    def build_mixer(turn, carry):
        start_row = pl.multiple_of(turn * GROUP * tall, 16)
        picked = jnp.dot(
            shifts[pl.ds(start_row, GROUP * tall), :],
            chosen[...],
            preferred_element_type=jnp.float32,
        )
        for member in range(GROUP):
            mixed = picked[member * tall : (member + 1) * tall] * coef_rows[
                pl.ds(turn * GROUP + member, 1), :
            ]
            mixer[pl.ds(pl.multiple_of(start_row + member * tall, 16), tall), :] = mixed.astype(
                jnp.bfloat16
            )
        return carry

    lax.fori_loop(0, channels // GROUP, build_mixer, 0)

    def wait_keep(step, carry):
        tx, tlo = member_of(step)
        keep_copy(own_member, tx * INNER + tlo, (tx, hi * INNER + tlo)).wait_recv()
        return carry

    lax.fori_loop(1, members, wait_keep, 0)
    for plane in range(planes):
        part_send[plane] = jnp.dot(
            plane_rows[plane * patch_rows : (plane + 1) * patch_rows],
            keep_recv[:, plane].reshape(members * rows, width),
            preferred_element_type=jnp.float32,
        ).astype(jnp.bfloat16)
    part_recv[hi] = part_send[hi]

    def wait_block(step, carry):
        tx, thi, tlo = partner(step)
        ty = thi * INNER + tlo
        block_copy(me, tx * ny + ty, (tx, ty)).wait_recv()
        return carry

    lax.fori_loop(0, count - 1, wait_block, 0)

    def plane_at(step):
        return lax.rem(hi + step, planes)

    def start_part(step, carry):
        thi = plane_at(step)
        part_copy(thi, hi, (mx, thi * INNER + lo)).start()
        return carry

    lax.fori_loop(1, planes, start_part, 0)
    arrived = recv[...].reshape(deep, width)
    for turn in range(channels // GROUP):
        mixed = jnp.dot(
            mixer[turn * GROUP * tall : (turn + 1) * GROUP * tall],
            arrived,
            preferred_element_type=jnp.float32,
        ).astype(jnp.bfloat16)
        for member in range(GROUP):
            channel = turn * GROUP + member
            for t in range(tiles):
                mixed_tiles[
                    t * tall : (t + 1) * tall, channel * LANES : (channel + 1) * LANES
                ] = mixed[member * tall : (member + 1) * tall, t * LANES : (t + 1) * LANES]
    summed = jnp.dot(mixed_tiles[...], bands[...], preferred_element_type=jnp.float32)
    zeros = jnp.zeros((tall, LANES), jnp.float32)
    now = [summed[t * tall : (t + 1) * tall, :LANES] for t in range(tiles)] + [zeros]
    after = [zeros] + [summed[t * tall : (t + 1) * tall, LANES:] for t in range(tiles)]
    joined = jnp.concatenate([a + b for a, b in zip(now, after)], axis=1)
    ext[...] = pltpu.roll(joined, width + LANES - margin, 1)

    top, middle, bottom = pl.ds(0, spill), pl.ds(spill, patch_rows), pl.ds(spill + patch_rows, spill)
    side, body_cols = pl.ds(width, LANES), pl.ds(0, width)
    plan = [
        (0, -1, (top, body_cols), edge_rows.at[1]),
        (0, 1, (bottom, body_cols), edge_rows.at[0]),
        (-1, 0, (middle, side), edge_cols.at[1]),
        (1, 0, (middle, side), edge_cols.at[0]),
        (-1, -1, (top, side), edge_corners.at[3]),
        (1, -1, (top, side), edge_corners.at[2]),
        (-1, 1, (bottom, side), edge_corners.at[1]),
        (1, 1, (bottom, side), edge_corners.at[0]),
    ]

    def exists(dx, dy):
        return (mx + dx >= 0) & (mx + dx < nx) & (my + dy >= 0) & (my + dy < ny)

    def edge_copy(number):
        dx, dy, piece, landing = plan[number]
        return pltpu.make_async_remote_copy(
            src_ref=ext.at[piece],
            dst_ref=landing,
            send_sem=edge_send_sem.at[number],
            recv_sem=edge_recv_sem.at[number],
            device_id=(mx + dx, my + dy),
            device_id_type=MESH,
        )

    for number, (dx, dy, _, _) in enumerate(plan):

        @pl.when(exists(dx, dy))
        def _():
            edge_copy(number).start()

    coadd_ref[...] = ext[middle, body_cols]

    def wait_part(step, carry):
        thi = plane_at(step)
        part_copy(hi, thi, (mx, thi * INNER + lo)).wait_recv()
        return carry

    lax.fori_loop(1, planes, wait_part, 0)
    weights = part_recv[0].astype(jnp.float32)
    for plane in range(1, planes):
        weights = weights + part_recv[plane].astype(jnp.float32)
    weight_ref[...] = weights

    lane = lax.broadcasted_iota(jnp.int32, (spill, LANES), 1)
    lane_tall = lax.broadcasted_iota(jnp.int32, (patch_rows, LANES), 1)
    low_rows, high_rows = pl.ds(0, spill), pl.ds(patch_rows - spill, spill)
    left, right = pl.ds(0, LANES), pl.ds(width - LANES, LANES)

    def from_side(value, lanes, dx):
        if dx < 0:
            return jnp.where(lanes < margin, value, 0.0)
        return jnp.where(lanes >= LANES - margin, value, 0.0)

    for number, (dx, dy, _, landing) in enumerate(plan):
        @pl.when(exists(-dx, -dy))
        def _():
            edge_copy(number).wait_recv()
            if dx == 0:
                here = low_rows if dy > 0 else high_rows
                coadd_ref[here, :] += landing[...]
            elif dy == 0:
                here = left if dx > 0 else right
                coadd_ref[:, here] += from_side(landing[...], lane_tall, -dx)
            else:
                here = (low_rows if dy > 0 else high_rows, left if dx > 0 else right)
                coadd_ref[here] += from_side(landing[...], lane, -dx)

    def sent_block(step, carry):
        tx, thi, tlo = partner(step)
        ty = thi * INNER + tlo
        block_copy(tx * ny + ty, me, (tx, ty)).wait_send()
        return carry

    def sent_keep(step, carry):
        tx, tlo = member_of(step)
        keep_copy(tx * INNER + tlo, own_member, (tx, hi * INNER + tlo)).wait_send()
        return carry

    def sent_part(step, carry):
        thi = plane_at(step)
        part_copy(thi, hi, (mx, thi * INNER + lo)).wait_send()
        return carry

    lax.fori_loop(0, count - 1, sent_block, 0)
    lax.fori_loop(1, members, sent_keep, 0)
    lax.fori_loop(1, planes, sent_part, 0)
    for number, (dx, dy, _, _) in enumerate(plan):

        @pl.when(exists(dx, dy))
        def _():
            edge_copy(number).wait_send()


def body(
    image, inverse_var, patch_of, row_of, valid, coef_index, coef_table, basis_across, basis_down
):
    nx, ny = lax.axis_size("skyx"), lax.axis_size("skyy")
    count = nx * ny
    planes, members = ny // INNER, nx * INNER
    blocks, rows, width = image.shape
    channels, taps = basis_across.shape
    margin = (taps - 1) // 2
    patch_rows = RS * rows
    spill = margin + LEAD
    tall = patch_rows + 2 * spill
    tiles = width // LANES
    deep = count * rows
    wide = count * blocks

    vmem = pl.BlockSpec(memory_space=pltpu.VMEM)
    operands = [
        image,
        inverse_var,
        patch_of.reshape(1, wide),
        row_of.reshape(1, wide),
        valid.reshape(1, wide),
        coef_index.reshape(1, count),
        coef_table.T,
        basis_across,
        basis_down,
    ]
    in_hbm = pl.BlockSpec(memory_space=pltpu.HBM)
    dma = pltpu.SemaphoreType.DMA
    return pl.pallas_call(
        functools.partial(kernel, nx, ny, taps),
        out_shape=(
            jax.ShapeDtypeStruct((patch_rows, width), jnp.float32),
            jax.ShapeDtypeStruct((patch_rows, width), jnp.float32),
        ),
        in_specs=[in_hbm] * len(operands),
        out_specs=(vmem, vmem),
        scratch_shapes=[
            pltpu.VMEM((blocks, rows, width), jnp.bfloat16),
            pltpu.VMEM((blocks, rows, width), jnp.bfloat16),
            pltpu.SMEM((1, wide), jnp.int32),
            pltpu.VMEM((1, wide), jnp.int32),
            pltpu.VMEM((1, wide), jnp.int32),
            pltpu.VMEM((1, wide), jnp.int32),
            pltpu.VMEM((1, count), jnp.int32),
            pltpu.VMEM(coef_table.shape[::-1], jnp.float32),
            pltpu.VMEM((channels, taps), jnp.float32),
            pltpu.VMEM((channels, taps), jnp.float32),
            pltpu.VMEM((count, rows, width), jnp.bfloat16),
            pltpu.VMEM((count, rows, width), jnp.bfloat16),
            pltpu.VMEM((members, planes, rows, width), jnp.bfloat16),
            pltpu.VMEM((members, planes, rows, width), jnp.bfloat16),
            pltpu.VMEM((planes, patch_rows, width), jnp.bfloat16),
            pltpu.VMEM((planes, patch_rows, width), jnp.bfloat16),
            pltpu.VMEM((channels, LANES), jnp.float32),
            pltpu.VMEM((channels, LANES), jnp.float32),
            pltpu.VMEM((channels, deep), jnp.float32),
            pltpu.VMEM((2 * patch_rows, deep), jnp.bfloat16),
            pltpu.VMEM((channels * LANES, 2 * LANES), jnp.bfloat16),
            pltpu.VMEM((channels * tall, LANES), jnp.bfloat16),
            pltpu.VMEM((channels * tall, deep), jnp.bfloat16),
            pltpu.VMEM((tiles * tall, channels * LANES), jnp.bfloat16),
            pltpu.VMEM((tall, width + LANES), jnp.float32),
            pltpu.VMEM((2, spill, width), jnp.float32),
            pltpu.VMEM((2, patch_rows, LANES), jnp.float32),
            pltpu.VMEM((4, spill, LANES), jnp.float32),
            dma((10,)),
            dma((count,)),
            dma((count,)),
            dma((members,)),
            dma((members,)),
            dma((planes,)),
            dma((planes,)),
            dma((8,)),
            dma((8,)),
        ],
        compiler_params=pltpu.CompilerParams(
            collective_id=0, has_side_effects=True, vmem_limit_bytes=(16 * 1024 + 256 * count) * 1024
        ),
    )(*[pltpu.with_memory_space_constraint(operand, pltpu.HBM) for operand in operands])


def solution(mesh):
    placed = (
        P(("skyx", "skyy"), None, None),
        P(("skyx", "skyy"), None, None),
        P(),
        P(),
        P(),
        P(),
        P(),
        P(),
        P(),
    )
    return jax.shard_map(
        body,
        mesh=mesh,
        in_specs=placed,
        out_specs=(P("skyy", "skyx"), P("skyy", "skyx")),
        check_vma=False,
    )
```

```python
import functools

import jax
import jax.numpy as jnp
from jax import lax
from jax.experimental import pallas as pl
from jax.experimental.pallas import tpu as pltpu
from jax.sharding import PartitionSpec as P

RS = 4
LANES = 128
LEAD = 4
INNER = 2
GROUP = 4
MESH = pl.DeviceIdType.MESH


def kernel(
    nx,
    ny,
    taps,
    image_hbm,
    ivar_hbm,
    patch_hbm,
    row_hbm,
    valid_hbm,
    sets_hbm,
    table_hbm,
    across_hbm,
    down_hbm,
    coadd_ref,
    weight_ref,
    image_ref,
    ivar_ref,
    patch_scalars,
    patch_lanes,
    row_lanes,
    valid_lanes,
    sets_lanes,
    table_ref,
    across_ref,
    down_ref,
    send,
    recv,
    keep_send,
    keep_recv,
    part_send,
    pair_recv,
    merged,
    part_recv,
    across_pad,
    down_pad,
    coef_rows,
    chosen,
    bands,
    shifts,
    mixer,
    mixed_tiles,
    ext,
    edge_rows,
    edge_cols,
    edge_corners,
    load_sem,
    send_sem,
    recv_sem,
    keep_send_sem,
    keep_recv_sem,
    pair_sem,
    part_send_sem,
    part_recv_sem,
    edge_send_sem,
    edge_recv_sem,
):
    count = nx * ny
    planes = ny // INNER
    members = nx * INNER
    blocks, rows, width = image_ref.shape
    patch_rows = RS * rows
    channels = across_ref.shape[0]
    margin = (taps - 1) // 2
    tall = ext.shape[0]
    tiles = width // LANES
    spill = margin + LEAD
    mx = lax.axis_index("skyx")
    my = lax.axis_index("skyy")
    me = mx * ny + my
    hi, lo = my // INNER, lax.rem(my, INNER)

    def partner(step):
        back = count - 1 - step
        tx = lax.rem(mx + lax.rem(back // INNER, nx), nx)
        thi = lax.rem(hi + back // members, planes)
        tlo = lax.rem(lo + lax.rem(back, INNER), INNER)
        return tx, thi, tlo

    barrier = pltpu.get_barrier_semaphore()
    pairs = [
        (patch_hbm, patch_scalars),
        (image_hbm, image_ref),
        (ivar_hbm, ivar_ref),
        (patch_hbm, patch_lanes),
        (row_hbm, row_lanes),
        (valid_hbm, valid_lanes),
        (sets_hbm, sets_lanes),
        (table_hbm, table_ref),
        (across_hbm, across_ref),
        (down_hbm, down_ref),
    ]
    loads = [
        pltpu.make_async_copy(source, landing, load_sem.at[number])
        for number, (source, landing) in enumerate(pairs)
    ]
    for load in loads:
        load.start()

    def greet(step, carry):
        tx, thi, tlo = partner(step)
        pl.semaphore_signal(
            barrier, inc=1, device_id=(tx, thi * INNER + tlo), device_id_type=MESH
        )
        return carry

    lax.fori_loop(0, count - 1, greet, 0)
    for load in loads[:3]:
        load.wait()
    targets = [patch_scalars[0, me * blocks + k] for k in range(blocks)]

    def stage(tx, thi, tlo):
        patch = tx * ny + thi * INNER + tlo
        block = 0
        for k in range(1, blocks):
            block = jnp.where(targets[k] == patch, k, block)
        weight = ivar_ref[block]
        product = weight.astype(jnp.float32) * image_ref[block].astype(jnp.float32)
        send[patch] = product.astype(jnp.bfloat16)
        keep_send[tx * INNER + tlo, thi] = weight

    def block_copy(target, source, device):
        return pltpu.make_async_remote_copy(
            src_ref=send.at[target],
            dst_ref=recv.at[source],
            send_sem=send_sem.at[target],
            recv_sem=recv_sem.at[source],
            device_id=device,
            device_id_type=MESH,
        )

    def keep_copy(target, source, device):
        return pltpu.make_async_remote_copy(
            src_ref=keep_send.at[target],
            dst_ref=keep_recv.at[source],
            send_sem=keep_send_sem.at[target],
            recv_sem=keep_recv_sem.at[source],
            device_id=device,
            device_id_type=MESH,
        )

    half = planes // 2
    parity, rank = lax.rem(hi, 2), hi // 2

    def pair_copy():
        return pltpu.make_async_remote_copy(
            src_ref=part_send.at[1 - parity],
            dst_ref=pair_recv,
            send_sem=pair_sem.at[0],
            recv_sem=pair_sem.at[1],
            device_id=(mx, (hi + 1 - 2 * parity) * INNER + lo),
            device_id_type=MESH,
        )

    def part_copy(target, source, device):
        return pltpu.make_async_remote_copy(
            src_ref=merged.at[target],
            dst_ref=part_recv.at[source],
            send_sem=part_send_sem.at[target],
            recv_sem=part_recv_sem.at[source],
            device_id=device,
            device_id_type=MESH,
        )

    def prepare(step, carry):
        stage(*partner(step))
        return carry

    lax.fori_loop(0, count, prepare, 0)
    pl.semaphore_wait(barrier, count - 1)

    def start(step, carry):
        tx, thi, tlo = partner(step)
        ty = thi * INNER + tlo
        block_copy(tx * ny + ty, me, (tx, ty)).start()
        return carry

    lax.fori_loop(0, count - members, start, 0)

    def member_of(step):
        return lax.rem(mx + step // INNER, nx), lax.rem(lo + lax.rem(step, INNER), INNER)

    own_member = mx * INNER + lo

    def start_keep(step, carry):
        tx, tlo = member_of(step)
        keep_copy(tx * INNER + tlo, own_member, (tx, hi * INNER + tlo)).start()
        return carry

    lax.fori_loop(1, members, start_keep, 0)
    lax.fori_loop(count - members, count - 1, start, 0)
    recv[me] = send[me]
    keep_recv[own_member] = keep_send[own_member]
    for load in loads[3:]:
        load.wait()

    def same(condition):
        return condition.astype(jnp.float32).astype(jnp.bfloat16)

    def iota(shape, dim):
        return lax.broadcasted_iota(jnp.int32, shape, dim)

    def over(value, by):
        return value >> (by.bit_length() - 1) if by & (by - 1) == 0 else value // by

    def within(value, by):
        return value & (by - 1) if by & (by - 1) == 0 else lax.rem(value, by)

    def spread(slots, groups):
        lanes = slots.shape[1]
        tall_flags = jnp.concatenate(
            [jnp.broadcast_to(slots[s : s + 1], (rows, lanes)) for s in range(groups * RS)], axis=0
        )
        shape = tall_flags.shape
        keep = within(iota(shape, 0), rows) == within(iota(shape, 1), rows)
        return jnp.where(keep, tall_flags, 0.0).astype(jnp.bfloat16)

    spot = jnp.where(valid_lanes[...] > 0, patch_lanes[...] * RS + row_lanes[...], -1)
    wide = count * blocks
    own_slots = same(iota((8, wide), 0) + me * RS == spot)
    own_slots = jnp.where(iota((8, wide), 0) < RS, own_slots, jnp.bfloat16(0))
    chunk = LANES // rows
    repeat = same(
        over(iota((chunk * blocks, LANES), 0), blocks) == over(iota((chunk * blocks, LANES), 1), rows)
    )
    own_flags = jnp.concatenate(
        [
            jnp.dot(
                own_slots[:, g * chunk * blocks : (g + 1) * chunk * blocks],
                repeat,
                preferred_element_type=jnp.float32,
            )
            for g in range(count // chunk)
        ],
        axis=1,
    )
    own_rows = spread(own_flags, 1)
    chosen[:patch_rows] = own_rows
    chosen[patch_rows:] = own_rows

    onehot = (iota((table_ref.shape[1], count), 0) == sets_lanes[...]).astype(jnp.float32)
    coeffs = jnp.dot(
        table_ref[...],
        onehot,
        precision=lax.Precision.HIGHEST,
        preferred_element_type=jnp.float32,
    )
    deep = count * rows
    coef_rows[...] = jnp.dot(
        coeffs,
        (iota((count, deep), 0) == over(iota((count, deep), 1), rows)).astype(jnp.float32),
        precision=lax.Precision.HIGHEST,
        preferred_element_type=jnp.float32,
    )

    shape = (planes * RS, wide)
    wanted = (mx * ny + over(iota(shape, 0), RS) * INNER + lo) * RS + within(iota(shape, 0), RS)
    shape = (wide, members * rows)
    member = over(iota(shape, 1), rows)
    exposure = over(member, INNER) * ny + hi * INNER + within(member, INNER)
    plane_flags = jnp.dot(
        same(wanted == spot),
        same(over(iota(shape, 0), blocks) == exposure),
        preferred_element_type=jnp.float32,
    )
    plane_rows = spread(plane_flags, planes)

    tap = iota((taps, LANES), 0)
    lane = iota((taps, LANES), 1)

    def laid(filters, where_to):
        return jnp.dot(
            filters,
            (lane == where_to).astype(jnp.float32),
            precision=lax.Precision.HIGHEST,
            preferred_element_type=jnp.float32,
        )

    across_pad[...] = laid(across_ref[...], tap)
    down_pad[...] = laid(down_ref[...], LANES - LEAD - tap)
    forward = iota((LANES, LANES), 1) >= iota((LANES, LANES), 0)
    first_half = iota((tall, LANES), 1) < patch_rows

    def build_bands(channel, carry):
        row = jnp.broadcast_to(across_pad[pl.ds(channel, 1), :], (LANES, LANES))
        band = pltpu.roll(row, 0, 1, stride=1, stride_axis=0)
        start_row = pl.multiple_of(channel * LANES, LANES)
        bands[pl.ds(start_row, LANES), :LANES] = jnp.where(forward, band, 0.0).astype(jnp.bfloat16)
        bands[pl.ds(start_row, LANES), LANES:] = jnp.where(forward, 0.0, band).astype(jnp.bfloat16)
        row = jnp.broadcast_to(down_pad[pl.ds(channel, 1), :], (tall, LANES))
        shifted = pltpu.roll(row, 0, 1, stride=1, stride_axis=0)
        high = shifted.astype(jnp.bfloat16).astype(jnp.float32)
        low = pltpu.roll(shifted - high, patch_rows, 1)
        start_row = pl.multiple_of(channel * tall, 16)
        shifts[pl.ds(start_row, tall), :] = jnp.where(first_half, high, low).astype(jnp.bfloat16)
        return carry

    lax.fori_loop(0, channels, build_bands, 0, unroll=4)

    def build_mixer(turn, carry):
        start_row = pl.multiple_of(turn * GROUP * tall, 16)
        picked = jnp.dot(
            shifts[pl.ds(start_row, GROUP * tall), :],
            chosen[...],
            preferred_element_type=jnp.float32,
        )
        for member in range(GROUP):
            mixed = picked[member * tall : (member + 1) * tall] * coef_rows[
                pl.ds(turn * GROUP + member, 1), :
            ]
            mixer[pl.ds(pl.multiple_of(start_row + member * tall, 16), tall), :] = mixed.astype(
                jnp.bfloat16
            )
        return carry

    lax.fori_loop(0, channels // GROUP, build_mixer, 0)

    def wait_keep(step, carry):
        tx, tlo = member_of(step)
        keep_copy(own_member, tx * INNER + tlo, (tx, hi * INNER + tlo)).wait_recv()
        return carry

    lax.fori_loop(1, members, wait_keep, 0)
    for plane in range(planes):
        part_send[plane % 2, plane // 2] = jnp.dot(
            plane_rows[plane * patch_rows : (plane + 1) * patch_rows],
            keep_recv[:, plane].reshape(members * rows, width),
            preferred_element_type=jnp.float32,
        ).astype(jnp.bfloat16)
    pair_copy().start()

    def wait_block(step, carry):
        tx, thi, tlo = partner(step)
        ty = thi * INNER + tlo
        block_copy(me, tx * ny + ty, (tx, ty)).wait_recv()
        return carry

    lax.fori_loop(0, count - 1, wait_block, 0)

    pair_copy().wait_recv()
    for place in range(half):
        merged[place] = (
            part_send[parity, place].astype(jnp.float32) + pair_recv[place].astype(jnp.float32)
        ).astype(jnp.bfloat16)
    part_recv[rank] = merged[rank]

    def rank_at(step):
        return lax.rem(rank + step, half)

    def device_at(place):
        return (mx, (place * 2 + parity) * INNER + lo)

    def start_part(step, carry):
        place = rank_at(step)
        part_copy(place, rank, device_at(place)).start()
        return carry

    lax.fori_loop(1, half, start_part, 0)
    arrived = recv[...].reshape(deep, width)
    for turn in range(channels // GROUP):
        mixed = jnp.dot(
            mixer[turn * GROUP * tall : (turn + 1) * GROUP * tall],
            arrived,
            preferred_element_type=jnp.float32,
        ).astype(jnp.bfloat16)
        for member in range(GROUP):
            channel = turn * GROUP + member
            for t in range(tiles):
                mixed_tiles[
                    t * tall : (t + 1) * tall, channel * LANES : (channel + 1) * LANES
                ] = mixed[member * tall : (member + 1) * tall, t * LANES : (t + 1) * LANES]
    summed = jnp.dot(mixed_tiles[...], bands[...], preferred_element_type=jnp.float32)
    zeros = jnp.zeros((tall, LANES), jnp.float32)
    now = [summed[t * tall : (t + 1) * tall, :LANES] for t in range(tiles)] + [zeros]
    after = [zeros] + [summed[t * tall : (t + 1) * tall, LANES:] for t in range(tiles)]
    joined = jnp.concatenate([a + b for a, b in zip(now, after)], axis=1)
    ext[...] = pltpu.roll(joined, width + LANES - margin, 1)

    top, middle, bottom = pl.ds(0, spill), pl.ds(spill, patch_rows), pl.ds(spill + patch_rows, spill)
    side, body_cols = pl.ds(width, LANES), pl.ds(0, width)
    plan = [
        (0, -1, (top, body_cols), edge_rows.at[1]),
        (0, 1, (bottom, body_cols), edge_rows.at[0]),
        (-1, 0, (middle, side), edge_cols.at[1]),
        (1, 0, (middle, side), edge_cols.at[0]),
        (-1, -1, (top, side), edge_corners.at[3]),
        (1, -1, (top, side), edge_corners.at[2]),
        (-1, 1, (bottom, side), edge_corners.at[1]),
        (1, 1, (bottom, side), edge_corners.at[0]),
    ]

    def exists(dx, dy):
        return (mx + dx >= 0) & (mx + dx < nx) & (my + dy >= 0) & (my + dy < ny)

    def edge_copy(number):
        dx, dy, piece, landing = plan[number]
        return pltpu.make_async_remote_copy(
            src_ref=ext.at[piece],
            dst_ref=landing,
            send_sem=edge_send_sem.at[number],
            recv_sem=edge_recv_sem.at[number],
            device_id=(mx + dx, my + dy),
            device_id_type=MESH,
        )

    for number, (dx, dy, _, _) in enumerate(plan):

        @pl.when(exists(dx, dy))
        def _():
            edge_copy(number).start()

    coadd_ref[...] = ext[middle, body_cols]

    def sent_block(step, carry):
        tx, thi, tlo = partner(step)
        ty = thi * INNER + tlo
        block_copy(tx * ny + ty, me, (tx, ty)).wait_send()
        return carry

    def sent_keep(step, carry):
        tx, tlo = member_of(step)
        keep_copy(tx * INNER + tlo, own_member, (tx, hi * INNER + tlo)).wait_send()
        return carry

    def sent_part(step, carry):
        place = rank_at(step)
        part_copy(place, rank, device_at(place)).wait_send()
        return carry

    lax.fori_loop(0, count - 1, sent_block, 0)
    lax.fori_loop(1, members, sent_keep, 0)
    pair_copy().wait_send()
    lax.fori_loop(1, half, sent_part, 0)
    def wait_part(step, carry):
        place = rank_at(step)
        part_copy(rank, place, device_at(place)).wait_recv()
        return carry

    lax.fori_loop(1, half, wait_part, 0)
    weights = part_recv[0].astype(jnp.float32)
    for place in range(1, half):
        weights = weights + part_recv[place].astype(jnp.float32)
    weight_ref[...] = weights

    lane = lax.broadcasted_iota(jnp.int32, (spill, LANES), 1)
    lane_tall = lax.broadcasted_iota(jnp.int32, (patch_rows, LANES), 1)
    low_rows, high_rows = pl.ds(0, spill), pl.ds(patch_rows - spill, spill)
    left, right = pl.ds(0, LANES), pl.ds(width - LANES, LANES)

    def from_side(value, lanes, dx):
        if dx < 0:
            return jnp.where(lanes < margin, value, 0.0)
        return jnp.where(lanes >= LANES - margin, value, 0.0)

    for number, (dx, dy, _, landing) in enumerate(plan):
        @pl.when(exists(-dx, -dy))
        def _():
            edge_copy(number).wait_recv()
            if dx == 0:
                here = low_rows if dy > 0 else high_rows
                coadd_ref[here, :] += landing[...]
            elif dy == 0:
                here = left if dx > 0 else right
                coadd_ref[:, here] += from_side(landing[...], lane_tall, -dx)
            else:
                here = (low_rows if dy > 0 else high_rows, left if dx > 0 else right)
                coadd_ref[here] += from_side(landing[...], lane, -dx)

    for number, (dx, dy, _, _) in enumerate(plan):

        @pl.when(exists(dx, dy))
        def _():
            edge_copy(number).wait_send()


def body(
    image, inverse_var, patch_of, row_of, valid, coef_index, coef_table, basis_across, basis_down
):
    nx, ny = lax.axis_size("skyx"), lax.axis_size("skyy")
    count = nx * ny
    planes, members = ny // INNER, nx * INNER
    blocks, rows, width = image.shape
    channels, taps = basis_across.shape
    margin = (taps - 1) // 2
    patch_rows = RS * rows
    spill = margin + LEAD
    tall = patch_rows + 2 * spill
    tiles = width // LANES
    deep = count * rows
    wide = count * blocks

    vmem = pl.BlockSpec(memory_space=pltpu.VMEM)
    operands = [
        image,
        inverse_var,
        patch_of.reshape(1, wide),
        row_of.reshape(1, wide),
        valid.reshape(1, wide),
        coef_index.reshape(1, count),
        coef_table.T,
        basis_across,
        basis_down,
    ]
    in_hbm = pl.BlockSpec(memory_space=pltpu.HBM)
    dma = pltpu.SemaphoreType.DMA
    return pl.pallas_call(
        functools.partial(kernel, nx, ny, taps),
        out_shape=(
            jax.ShapeDtypeStruct((patch_rows, width), jnp.float32),
            jax.ShapeDtypeStruct((patch_rows, width), jnp.float32),
        ),
        in_specs=[in_hbm] * len(operands),
        out_specs=(vmem, vmem),
        scratch_shapes=[
            pltpu.VMEM((blocks, rows, width), jnp.bfloat16),
            pltpu.VMEM((blocks, rows, width), jnp.bfloat16),
            pltpu.SMEM((1, wide), jnp.int32),
            pltpu.VMEM((1, wide), jnp.int32),
            pltpu.VMEM((1, wide), jnp.int32),
            pltpu.VMEM((1, wide), jnp.int32),
            pltpu.VMEM((1, count), jnp.int32),
            pltpu.VMEM(coef_table.shape[::-1], jnp.float32),
            pltpu.VMEM((channels, taps), jnp.float32),
            pltpu.VMEM((channels, taps), jnp.float32),
            pltpu.VMEM((count, rows, width), jnp.bfloat16),
            pltpu.VMEM((count, rows, width), jnp.bfloat16),
            pltpu.VMEM((members, planes, rows, width), jnp.bfloat16),
            pltpu.VMEM((members, planes, rows, width), jnp.bfloat16),
            pltpu.VMEM((2, planes // 2, patch_rows, width), jnp.bfloat16),
            pltpu.VMEM((planes // 2, patch_rows, width), jnp.bfloat16),
            pltpu.VMEM((planes // 2, patch_rows, width), jnp.bfloat16),
            pltpu.VMEM((planes // 2, patch_rows, width), jnp.bfloat16),
            pltpu.VMEM((channels, LANES), jnp.float32),
            pltpu.VMEM((channels, LANES), jnp.float32),
            pltpu.VMEM((channels, deep), jnp.float32),
            pltpu.VMEM((2 * patch_rows, deep), jnp.bfloat16),
            pltpu.VMEM((channels * LANES, 2 * LANES), jnp.bfloat16),
            pltpu.VMEM((channels * tall, LANES), jnp.bfloat16),
            pltpu.VMEM((channels * tall, deep), jnp.bfloat16),
            pltpu.VMEM((tiles * tall, channels * LANES), jnp.bfloat16),
            pltpu.VMEM((tall, width + LANES), jnp.float32),
            pltpu.VMEM((2, spill, width), jnp.float32),
            pltpu.VMEM((2, patch_rows, LANES), jnp.float32),
            pltpu.VMEM((4, spill, LANES), jnp.float32),
            dma((10,)),
            dma((count,)),
            dma((count,)),
            dma((members,)),
            dma((members,)),
            dma((2,)),
            dma((planes // 2,)),
            dma((planes // 2,)),
            dma((8,)),
            dma((8,)),
        ],
        compiler_params=pltpu.CompilerParams(
            collective_id=0, has_side_effects=True, vmem_limit_bytes=(16 * 1024 + 256 * count) * 1024
        ),
    )(*[pltpu.with_memory_space_constraint(operand, pltpu.HBM) for operand in operands])


def solution(mesh):
    placed = (
        P(("skyx", "skyy"), None, None),
        P(("skyx", "skyy"), None, None),
        P(),
        P(),
        P(),
        P(),
        P(),
        P(),
        P(),
    )
    return jax.shard_map(
        body,
        mesh=mesh,
        in_specs=placed,
        out_specs=(P("skyy", "skyx"), P("skyy", "skyx")),
        check_vma=False,
    )
```

```python
import functools

import jax
import jax.numpy as jnp
from jax import lax
from jax.experimental import pallas as pl
from jax.experimental.pallas import tpu as pltpu
from jax.sharding import PartitionSpec as P

RS = 4
LANES = 128
LEAD = 4
INNER = 2
GROUP = 4
MESH = pl.DeviceIdType.MESH


def kernel(
    nx,
    ny,
    taps,
    image_hbm,
    ivar_hbm,
    patch_hbm,
    row_hbm,
    valid_hbm,
    sets_hbm,
    table_hbm,
    across_hbm,
    down_hbm,
    coadd_ref,
    weight_ref,
    image_ref,
    ivar_ref,
    patch_scalars,
    picks,
    patch_lanes,
    row_lanes,
    valid_lanes,
    sets_lanes,
    table_ref,
    across_ref,
    down_ref,
    send,
    recv,
    keep_send,
    keep_recv,
    part_send,
    pair_recv,
    merged,
    part_recv,
    across_pad,
    down_pad,
    coef_rows,
    chosen,
    bands,
    shifts,
    mixer,
    mixed_tiles,
    ext,
    edge_rows,
    edge_cols,
    edge_corners,
    load_sem,
    send_sem,
    recv_sem,
    keep_send_sem,
    keep_recv_sem,
    pair_sem,
    part_send_sem,
    part_recv_sem,
    edge_send_sem,
    edge_recv_sem,
):
    count = nx * ny
    planes = ny // INNER
    members = nx * INNER
    blocks, rows, width = image_ref.shape
    patch_rows = RS * rows
    channels = across_ref.shape[0]
    margin = (taps - 1) // 2
    tall = ext.shape[0]
    tiles = width // LANES
    spill = margin + LEAD
    mx = lax.axis_index("skyx")
    my = lax.axis_index("skyy")
    me = mx * ny + my
    hi, lo = my // INNER, lax.rem(my, INNER)

    def partner(step):
        back = count - 1 - step
        tx = lax.rem(mx + lax.rem(back // INNER, nx), nx)
        thi = lax.rem(hi + back // members, planes)
        tlo = lax.rem(lo + lax.rem(back, INNER), INNER)
        return tx, thi, tlo

    barrier = pltpu.get_barrier_semaphore()
    pairs = [
        (patch_hbm, patch_scalars),
        (image_hbm, image_ref),
        (ivar_hbm, ivar_ref),
        (patch_hbm, patch_lanes),
        (row_hbm, row_lanes),
        (valid_hbm, valid_lanes),
        (sets_hbm, sets_lanes),
        (table_hbm, table_ref),
        (across_hbm, across_ref),
        (down_hbm, down_ref),
    ]
    loads = [
        pltpu.make_async_copy(source, landing, load_sem.at[number])
        for number, (source, landing) in enumerate(pairs)
    ]
    for load in loads:
        load.start()

    def greet(step, carry):
        tx, thi, tlo = partner(step)
        pl.semaphore_signal(
            barrier, inc=1, device_id=(tx, thi * INNER + tlo), device_id_type=MESH
        )
        return carry

    lax.fori_loop(0, count - 1, greet, 0)
    loads[0].wait()
    targets = [patch_scalars[0, me * blocks + k] for k in range(blocks)]

    def find(patch, carry):
        block = 0
        for k in range(1, blocks):
            block = jnp.where(targets[k] == patch, k, block)
        picks[patch] = block
        return carry

    lax.fori_loop(0, count, find, 0)
    for load in loads[1:3]:
        load.wait()

    def stage(tx, thi, tlo):
        patch = tx * ny + thi * INNER + tlo
        block = picks[patch]
        weight = ivar_ref[block]
        product = weight.astype(jnp.float32) * image_ref[block].astype(jnp.float32)
        send[patch] = product.astype(jnp.bfloat16)
        keep_send[tx * INNER + tlo, thi] = weight

    def block_copy(target, source, device):
        return pltpu.make_async_remote_copy(
            src_ref=send.at[target],
            dst_ref=recv.at[source],
            send_sem=send_sem.at[target],
            recv_sem=recv_sem.at[source],
            device_id=device,
            device_id_type=MESH,
        )

    def keep_copy(target, source, device):
        return pltpu.make_async_remote_copy(
            src_ref=keep_send.at[target],
            dst_ref=keep_recv.at[source],
            send_sem=keep_send_sem.at[target],
            recv_sem=keep_recv_sem.at[source],
            device_id=device,
            device_id_type=MESH,
        )

    half = planes // 2
    parity, rank = lax.rem(hi, 2), hi // 2

    def pair_copy():
        return pltpu.make_async_remote_copy(
            src_ref=part_send.at[1 - parity],
            dst_ref=pair_recv,
            send_sem=pair_sem.at[0],
            recv_sem=pair_sem.at[1],
            device_id=(mx, (hi + 1 - 2 * parity) * INNER + lo),
            device_id_type=MESH,
        )

    def part_copy(target, source, device):
        return pltpu.make_async_remote_copy(
            src_ref=merged.at[target],
            dst_ref=part_recv.at[source],
            send_sem=part_send_sem.at[target],
            recv_sem=part_recv_sem.at[source],
            device_id=device,
            device_id_type=MESH,
        )

    def prepare(step, carry):
        stage(*partner(step))
        return carry

    lax.fori_loop(0, count, prepare, 0)
    pl.semaphore_wait(barrier, count - 1)

    def start(step, carry):
        tx, thi, tlo = partner(step)
        ty = thi * INNER + tlo
        block_copy(tx * ny + ty, me, (tx, ty)).start()
        return carry

    lax.fori_loop(0, count - members, start, 0)

    def member_of(step):
        return lax.rem(mx + step // INNER, nx), lax.rem(lo + lax.rem(step, INNER), INNER)

    own_member = mx * INNER + lo

    def start_keep(step, carry):
        tx, tlo = member_of(step)
        keep_copy(tx * INNER + tlo, own_member, (tx, hi * INNER + tlo)).start()
        return carry

    lax.fori_loop(1, members, start_keep, 0)
    lax.fori_loop(count - members, count - 1, start, 0)
    recv[me] = send[me]
    keep_recv[own_member] = keep_send[own_member]
    for load in loads[3:]:
        load.wait()

    def same(condition):
        return condition.astype(jnp.float32).astype(jnp.bfloat16)

    def iota(shape, dim):
        return lax.broadcasted_iota(jnp.int32, shape, dim)

    def over(value, by):
        return value >> (by.bit_length() - 1) if by & (by - 1) == 0 else value // by

    def within(value, by):
        return value & (by - 1) if by & (by - 1) == 0 else lax.rem(value, by)

    def spread(slots, groups):
        lanes = slots.shape[1]
        tall_flags = jnp.concatenate(
            [jnp.broadcast_to(slots[s : s + 1], (rows, lanes)) for s in range(groups * RS)], axis=0
        )
        shape = tall_flags.shape
        keep = within(iota(shape, 0), rows) == within(iota(shape, 1), rows)
        return jnp.where(keep, tall_flags, 0.0).astype(jnp.bfloat16)

    spot = jnp.where(valid_lanes[...] > 0, patch_lanes[...] * RS + row_lanes[...], -1)
    wide = count * blocks
    own_slots = same(iota((8, wide), 0) + me * RS == spot)
    own_slots = jnp.where(iota((8, wide), 0) < RS, own_slots, jnp.bfloat16(0))
    chunk = LANES // rows
    repeat = same(
        over(iota((chunk * blocks, LANES), 0), blocks) == over(iota((chunk * blocks, LANES), 1), rows)
    )
    own_flags = jnp.concatenate(
        [
            jnp.dot(
                own_slots[:, g * chunk * blocks : (g + 1) * chunk * blocks],
                repeat,
                preferred_element_type=jnp.float32,
            )
            for g in range(count // chunk)
        ],
        axis=1,
    )
    own_rows = spread(own_flags, 1)
    chosen[:patch_rows] = own_rows
    chosen[patch_rows:] = own_rows

    onehot = (iota((table_ref.shape[1], count), 0) == sets_lanes[...]).astype(jnp.float32)
    coeffs = jnp.dot(
        table_ref[...],
        onehot,
        precision=lax.Precision.HIGHEST,
        preferred_element_type=jnp.float32,
    )
    deep = count * rows
    coef_rows[...] = jnp.dot(
        coeffs,
        (iota((count, deep), 0) == over(iota((count, deep), 1), rows)).astype(jnp.float32),
        precision=lax.Precision.HIGHEST,
        preferred_element_type=jnp.float32,
    )

    shape = (planes * RS, wide)
    wanted = (mx * ny + over(iota(shape, 0), RS) * INNER + lo) * RS + within(iota(shape, 0), RS)
    shape = (wide, members * rows)
    member = over(iota(shape, 1), rows)
    exposure = over(member, INNER) * ny + hi * INNER + within(member, INNER)
    plane_flags = jnp.dot(
        same(wanted == spot),
        same(over(iota(shape, 0), blocks) == exposure),
        preferred_element_type=jnp.float32,
    )
    plane_rows = spread(plane_flags, planes)

    tap = iota((taps, LANES), 0)
    lane = iota((taps, LANES), 1)

    def laid(filters, where_to):
        return jnp.dot(
            filters,
            (lane == where_to).astype(jnp.float32),
            precision=lax.Precision.HIGHEST,
            preferred_element_type=jnp.float32,
        )

    across_pad[...] = laid(across_ref[...], tap)
    down_pad[...] = laid(down_ref[...], LANES - LEAD - tap)
    forward = iota((LANES, LANES), 1) >= iota((LANES, LANES), 0)
    first_half = iota((tall, LANES), 1) < patch_rows

    def build_bands(channel, carry):
        row = jnp.broadcast_to(across_pad[pl.ds(channel, 1), :], (LANES, LANES))
        band = pltpu.roll(row, 0, 1, stride=1, stride_axis=0)
        start_row = pl.multiple_of(channel * LANES, LANES)
        bands[pl.ds(start_row, LANES), :LANES] = jnp.where(forward, band, 0.0).astype(jnp.bfloat16)
        bands[pl.ds(start_row, LANES), LANES:] = jnp.where(forward, 0.0, band).astype(jnp.bfloat16)
        row = jnp.broadcast_to(down_pad[pl.ds(channel, 1), :], (tall, LANES))
        shifted = pltpu.roll(row, 0, 1, stride=1, stride_axis=0)
        high = shifted.astype(jnp.bfloat16).astype(jnp.float32)
        low = pltpu.roll(shifted - high, patch_rows, 1)
        start_row = pl.multiple_of(channel * tall, 16)
        shifts[pl.ds(start_row, tall), :] = jnp.where(first_half, high, low).astype(jnp.bfloat16)
        return carry

    lax.fori_loop(0, channels, build_bands, 0, unroll=4)

    def build_mixer(turn, carry):
        start_row = pl.multiple_of(turn * GROUP * tall, 16)
        picked = jnp.dot(
            shifts[pl.ds(start_row, GROUP * tall), :],
            chosen[...],
            preferred_element_type=jnp.float32,
        )
        for member in range(GROUP):
            mixed = picked[member * tall : (member + 1) * tall] * coef_rows[
                pl.ds(turn * GROUP + member, 1), :
            ]
            mixer[pl.ds(pl.multiple_of(start_row + member * tall, 16), tall), :] = mixed.astype(
                jnp.bfloat16
            )
        return carry

    lax.fori_loop(0, channels // GROUP, build_mixer, 0)

    def wait_keep(step, carry):
        tx, tlo = member_of(step)
        keep_copy(own_member, tx * INNER + tlo, (tx, hi * INNER + tlo)).wait_recv()
        return carry

    lax.fori_loop(1, members, wait_keep, 0)
    for plane in range(planes):
        part_send[plane % 2, plane // 2] = jnp.dot(
            plane_rows[plane * patch_rows : (plane + 1) * patch_rows],
            keep_recv[:, plane].reshape(members * rows, width),
            preferred_element_type=jnp.float32,
        ).astype(jnp.bfloat16)
    pair_copy().start()

    def wait_block(step, carry):
        tx, thi, tlo = partner(step)
        ty = thi * INNER + tlo
        block_copy(me, tx * ny + ty, (tx, ty)).wait_recv()
        return carry

    lax.fori_loop(0, count - 1, wait_block, 0)

    arrived = recv[...].reshape(deep, width)
    for turn in range(channels // GROUP):
        mixed = jnp.dot(
            mixer[turn * GROUP * tall : (turn + 1) * GROUP * tall],
            arrived,
            preferred_element_type=jnp.float32,
        ).astype(jnp.bfloat16)
        for member in range(GROUP):
            channel = turn * GROUP + member
            for t in range(tiles):
                mixed_tiles[
                    t * tall : (t + 1) * tall, channel * LANES : (channel + 1) * LANES
                ] = mixed[member * tall : (member + 1) * tall, t * LANES : (t + 1) * LANES]
    summed = jnp.dot(mixed_tiles[...], bands[...], preferred_element_type=jnp.float32)
    zeros = jnp.zeros((tall, LANES), jnp.float32)
    now = [summed[t * tall : (t + 1) * tall, :LANES] for t in range(tiles)] + [zeros]
    after = [zeros] + [summed[t * tall : (t + 1) * tall, LANES:] for t in range(tiles)]
    joined = jnp.concatenate([a + b for a, b in zip(now, after)], axis=1)
    ext[...] = pltpu.roll(joined, width + LANES - margin, 1)

    top, middle, bottom = pl.ds(0, spill), pl.ds(spill, patch_rows), pl.ds(spill + patch_rows, spill)
    side, body_cols = pl.ds(width, LANES), pl.ds(0, width)
    plan = [
        (0, -1, (top, body_cols), edge_rows.at[1]),
        (0, 1, (bottom, body_cols), edge_rows.at[0]),
        (-1, 0, (middle, side), edge_cols.at[1]),
        (1, 0, (middle, side), edge_cols.at[0]),
        (-1, -1, (top, side), edge_corners.at[3]),
        (1, -1, (top, side), edge_corners.at[2]),
        (-1, 1, (bottom, side), edge_corners.at[1]),
        (1, 1, (bottom, side), edge_corners.at[0]),
    ]

    def exists(dx, dy):
        return (mx + dx >= 0) & (mx + dx < nx) & (my + dy >= 0) & (my + dy < ny)

    def edge_copy(number):
        dx, dy, piece, landing = plan[number]
        return pltpu.make_async_remote_copy(
            src_ref=ext.at[piece],
            dst_ref=landing,
            send_sem=edge_send_sem.at[number],
            recv_sem=edge_recv_sem.at[number],
            device_id=(mx + dx, my + dy),
            device_id_type=MESH,
        )

    for number, (dx, dy, _, _) in enumerate(plan):

        @pl.when(exists(dx, dy))
        def _():
            edge_copy(number).start()

    coadd_ref[...] = ext[middle, body_cols]

    pair_copy().wait_recv()
    for place in range(half):
        merged[place] = (
            part_send[parity, place].astype(jnp.float32) + pair_recv[place].astype(jnp.float32)
        ).astype(jnp.bfloat16)
    part_recv[rank] = merged[rank]

    def rank_at(step):
        return lax.rem(rank + step, half)

    def device_at(place):
        return (mx, (place * 2 + parity) * INNER + lo)

    def start_part(step, carry):
        place = rank_at(step)
        part_copy(place, rank, device_at(place)).start()
        return carry

    lax.fori_loop(1, half, start_part, 0)
    def sent_block(step, carry):
        tx, thi, tlo = partner(step)
        ty = thi * INNER + tlo
        block_copy(tx * ny + ty, me, (tx, ty)).wait_send()
        return carry

    def sent_keep(step, carry):
        tx, tlo = member_of(step)
        keep_copy(tx * INNER + tlo, own_member, (tx, hi * INNER + tlo)).wait_send()
        return carry

    lax.fori_loop(0, count - 1, sent_block, 0)
    lax.fori_loop(1, members, sent_keep, 0)
    pair_copy().wait_send()
    lane = lax.broadcasted_iota(jnp.int32, (spill, LANES), 1)
    lane_tall = lax.broadcasted_iota(jnp.int32, (patch_rows, LANES), 1)
    low_rows, high_rows = pl.ds(0, spill), pl.ds(patch_rows - spill, spill)
    left, right = pl.ds(0, LANES), pl.ds(width - LANES, LANES)

    def from_side(value, lanes, dx):
        if dx < 0:
            return jnp.where(lanes < margin, value, 0.0)
        return jnp.where(lanes >= LANES - margin, value, 0.0)

    for number, (dx, dy, _, landing) in enumerate(plan):
        @pl.when(exists(-dx, -dy))
        def _():
            edge_copy(number).wait_recv()
            if dx == 0:
                here = low_rows if dy > 0 else high_rows
                coadd_ref[here, :] += landing[...]
            elif dy == 0:
                here = left if dx > 0 else right
                coadd_ref[:, here] += from_side(landing[...], lane_tall, -dx)
            else:
                here = (low_rows if dy > 0 else high_rows, left if dx > 0 else right)
                coadd_ref[here] += from_side(landing[...], lane, -dx)

    def sent_part(step, carry):
        place = rank_at(step)
        part_copy(place, rank, device_at(place)).wait_send()
        return carry

    def wait_part(step, carry):
        place = rank_at(step)
        part_copy(rank, place, device_at(place)).wait_recv()
        return carry

    lax.fori_loop(1, half, wait_part, 0)
    weights = part_recv[0].astype(jnp.float32)
    for place in range(1, half):
        weights = weights + part_recv[place].astype(jnp.float32)
    weight_ref[...] = weights

    lax.fori_loop(1, half, sent_part, 0)
    for number, (dx, dy, _, _) in enumerate(plan):

        @pl.when(exists(dx, dy))
        def _():
            edge_copy(number).wait_send()


def body(
    image, inverse_var, patch_of, row_of, valid, coef_index, coef_table, basis_across, basis_down
):
    nx, ny = lax.axis_size("skyx"), lax.axis_size("skyy")
    count = nx * ny
    planes, members = ny // INNER, nx * INNER
    blocks, rows, width = image.shape
    channels, taps = basis_across.shape
    margin = (taps - 1) // 2
    patch_rows = RS * rows
    spill = margin + LEAD
    tall = patch_rows + 2 * spill
    tiles = width // LANES
    deep = count * rows
    wide = count * blocks

    vmem = pl.BlockSpec(memory_space=pltpu.VMEM)
    operands = [
        image,
        inverse_var,
        patch_of.reshape(1, wide),
        row_of.reshape(1, wide),
        valid.reshape(1, wide),
        coef_index.reshape(1, count),
        coef_table.T,
        basis_across,
        basis_down,
    ]
    in_hbm = pl.BlockSpec(memory_space=pltpu.HBM)
    dma = pltpu.SemaphoreType.DMA
    return pl.pallas_call(
        functools.partial(kernel, nx, ny, taps),
        out_shape=(
            jax.ShapeDtypeStruct((patch_rows, width), jnp.float32),
            jax.ShapeDtypeStruct((patch_rows, width), jnp.float32),
        ),
        in_specs=[in_hbm] * len(operands),
        out_specs=(vmem, vmem),
        scratch_shapes=[
            pltpu.VMEM((blocks, rows, width), jnp.bfloat16),
            pltpu.VMEM((blocks, rows, width), jnp.bfloat16),
            pltpu.SMEM((1, wide), jnp.int32),
            pltpu.SMEM((count,), jnp.int32),
            pltpu.VMEM((1, wide), jnp.int32),
            pltpu.VMEM((1, wide), jnp.int32),
            pltpu.VMEM((1, wide), jnp.int32),
            pltpu.VMEM((1, count), jnp.int32),
            pltpu.VMEM(coef_table.shape[::-1], jnp.float32),
            pltpu.VMEM((channels, taps), jnp.float32),
            pltpu.VMEM((channels, taps), jnp.float32),
            pltpu.VMEM((count, rows, width), jnp.bfloat16),
            pltpu.VMEM((count, rows, width), jnp.bfloat16),
            pltpu.VMEM((members, planes, rows, width), jnp.bfloat16),
            pltpu.VMEM((members, planes, rows, width), jnp.bfloat16),
            pltpu.VMEM((2, planes // 2, patch_rows, width), jnp.bfloat16),
            pltpu.VMEM((planes // 2, patch_rows, width), jnp.bfloat16),
            pltpu.VMEM((planes // 2, patch_rows, width), jnp.bfloat16),
            pltpu.VMEM((planes // 2, patch_rows, width), jnp.bfloat16),
            pltpu.VMEM((channels, LANES), jnp.float32),
            pltpu.VMEM((channels, LANES), jnp.float32),
            pltpu.VMEM((channels, deep), jnp.float32),
            pltpu.VMEM((2 * patch_rows, deep), jnp.bfloat16),
            pltpu.VMEM((channels * LANES, 2 * LANES), jnp.bfloat16),
            pltpu.VMEM((channels * tall, LANES), jnp.bfloat16),
            pltpu.VMEM((channels * tall, deep), jnp.bfloat16),
            pltpu.VMEM((tiles * tall, channels * LANES), jnp.bfloat16),
            pltpu.VMEM((tall, width + LANES), jnp.float32),
            pltpu.VMEM((2, spill, width), jnp.float32),
            pltpu.VMEM((2, patch_rows, LANES), jnp.float32),
            pltpu.VMEM((4, spill, LANES), jnp.float32),
            dma((10,)),
            dma((count,)),
            dma((count,)),
            dma((members,)),
            dma((members,)),
            dma((2,)),
            dma((planes // 2,)),
            dma((planes // 2,)),
            dma((8,)),
            dma((8,)),
        ],
        compiler_params=pltpu.CompilerParams(
            collective_id=0, has_side_effects=True, vmem_limit_bytes=(16 * 1024 + 256 * count) * 1024
        ),
    )(*[pltpu.with_memory_space_constraint(operand, pltpu.HBM) for operand in operands])


def solution(mesh):
    placed = (
        P(("skyx", "skyy"), None, None),
        P(("skyx", "skyy"), None, None),
        P(),
        P(),
        P(),
        P(),
        P(),
        P(),
        P(),
    )
    return jax.shard_map(
        body,
        mesh=mesh,
        in_specs=placed,
        out_specs=(P("skyy", "skyx"), P("skyy", "skyx")),
        check_vma=False,
    )
```

```python
import functools

import jax
import jax.numpy as jnp
from jax import lax
from jax.experimental import pallas as pl
from jax.experimental.pallas import tpu as pltpu
from jax.sharding import PartitionSpec as P

RS = 4
LANES = 128
LEAD = 4
INNER = 2
GROUP = 4
MESH = pl.DeviceIdType.MESH


def kernel(
    nx,
    ny,
    taps,
    image_hbm,
    ivar_hbm,
    patch_hbm,
    row_hbm,
    valid_hbm,
    sets_hbm,
    table_hbm,
    across_hbm,
    down_hbm,
    coadd_ref,
    weight_ref,
    image_ref,
    ivar_ref,
    patch_scalars,
    picks,
    patch_lanes,
    row_lanes,
    valid_lanes,
    sets_lanes,
    table_ref,
    across_ref,
    down_ref,
    send,
    recv,
    keep_send,
    keep_recv,
    part_send,
    pair_recv,
    merged,
    part_recv,
    across_pad,
    down_pad,
    coef_rows,
    chosen,
    bands,
    shifts,
    mixer,
    mixed_tiles,
    ext,
    edge_rows,
    edge_cols,
    edge_corners,
    load_sem,
    send_sem,
    recv_sem,
    keep_send_sem,
    keep_recv_sem,
    pair_sem,
    part_send_sem,
    part_recv_sem,
    edge_send_sem,
    edge_recv_sem,
):
    count = nx * ny
    planes = ny // INNER
    members = nx * INNER
    blocks, rows, width = image_ref.shape
    patch_rows = RS * rows
    channels = across_ref.shape[0]
    margin = (taps - 1) // 2
    tall = ext.shape[0]
    tiles = width // LANES
    spill = margin + LEAD
    mx = lax.axis_index("skyx")
    my = lax.axis_index("skyy")
    me = mx * ny + my
    hi, lo = my // INNER, lax.rem(my, INNER)

    def plane_across(distance):
        if planes & (planes - 1):
            return lax.rem(hi + distance, planes)
        plane = 0
        for bit in range(planes.bit_length() - 1):
            power = 1 << bit
            plane = plane + lax.rem(hi // power + distance // power, 2) * power
        return plane

    def partner(step):
        back = count - 1 - step
        tx = lax.rem(mx + lax.rem(back // INNER, nx), nx)
        thi = plane_across(back // members)
        tlo = lax.rem(lo + lax.rem(back, INNER), INNER)
        return tx, thi, tlo

    barrier = pltpu.get_barrier_semaphore()
    pairs = [
        (patch_hbm, patch_scalars),
        (image_hbm, image_ref),
        (ivar_hbm, ivar_ref),
        (patch_hbm, patch_lanes),
        (row_hbm, row_lanes),
        (valid_hbm, valid_lanes),
        (sets_hbm, sets_lanes),
        (table_hbm, table_ref),
        (across_hbm, across_ref),
        (down_hbm, down_ref),
    ]
    loads = [
        pltpu.make_async_copy(source, landing, load_sem.at[number])
        for number, (source, landing) in enumerate(pairs)
    ]
    for load in loads:
        load.start()

    def greet(step, carry):
        tx, thi, tlo = partner(step)
        pl.semaphore_signal(
            barrier, inc=1, device_id=(tx, thi * INNER + tlo), device_id_type=MESH
        )
        return carry

    lax.fori_loop(0, count - 1, greet, 0)
    loads[0].wait()
    targets = [patch_scalars[0, me * blocks + k] for k in range(blocks)]

    def find(patch, carry):
        block = 0
        for k in range(1, blocks):
            block = jnp.where(targets[k] == patch, k, block)
        picks[patch] = block
        return carry

    lax.fori_loop(0, count, find, 0)
    for load in loads[1:3]:
        load.wait()

    def stage(tx, thi, tlo):
        patch = tx * ny + thi * INNER + tlo
        block = picks[patch]
        weight = ivar_ref[block]
        product = weight.astype(jnp.float32) * image_ref[block].astype(jnp.float32)
        send[patch] = product.astype(jnp.bfloat16)
        keep_send[tx * INNER + tlo, thi] = weight

    def block_copy(target, source, device):
        return pltpu.make_async_remote_copy(
            src_ref=send.at[target],
            dst_ref=recv.at[source],
            send_sem=send_sem.at[target],
            recv_sem=recv_sem.at[source],
            device_id=device,
            device_id_type=MESH,
        )

    def keep_copy(target, source, device):
        return pltpu.make_async_remote_copy(
            src_ref=keep_send.at[target],
            dst_ref=keep_recv.at[source],
            send_sem=keep_send_sem.at[target],
            recv_sem=keep_recv_sem.at[source],
            device_id=device,
            device_id_type=MESH,
        )

    half = planes // 2
    parity, rank = lax.rem(hi, 2), hi // 2

    def pair_copy():
        return pltpu.make_async_remote_copy(
            src_ref=part_send.at[1 - parity],
            dst_ref=pair_recv,
            send_sem=pair_sem.at[0],
            recv_sem=pair_sem.at[1],
            device_id=(mx, (hi + 1 - 2 * parity) * INNER + lo),
            device_id_type=MESH,
        )

    def part_copy(target, source, device):
        return pltpu.make_async_remote_copy(
            src_ref=merged.at[target],
            dst_ref=part_recv.at[source],
            send_sem=part_send_sem.at[target],
            recv_sem=part_recv_sem.at[source],
            device_id=device,
            device_id_type=MESH,
        )

    def prepare(step, carry):
        stage(*partner(step))
        return carry

    lax.fori_loop(0, count, prepare, 0)
    pl.semaphore_wait(barrier, count - 1)

    def start(step, carry):
        tx, thi, tlo = partner(step)
        ty = thi * INNER + tlo
        block_copy(tx * ny + ty, me, (tx, ty)).start()
        return carry

    lax.fori_loop(0, count // 2, start, 0)

    def member_of(step):
        return lax.rem(mx + step // INNER, nx), lax.rem(lo + lax.rem(step, INNER), INNER)

    own_member = mx * INNER + lo

    def start_keep(step, carry):
        tx, tlo = member_of(step)
        keep_copy(tx * INNER + tlo, own_member, (tx, hi * INNER + tlo)).start()
        return carry

    lax.fori_loop(1, members, start_keep, 0)
    lax.fori_loop(count // 2, count - 1, start, 0)
    recv[me] = send[me]
    keep_recv[own_member] = keep_send[own_member]
    for load in loads[3:]:
        load.wait()

    def same(condition):
        return condition.astype(jnp.float32).astype(jnp.bfloat16)

    def iota(shape, dim):
        return lax.broadcasted_iota(jnp.int32, shape, dim)

    def over(value, by):
        return value >> (by.bit_length() - 1) if by & (by - 1) == 0 else value // by

    def within(value, by):
        return value & (by - 1) if by & (by - 1) == 0 else lax.rem(value, by)

    def spread(slots, groups):
        lanes = slots.shape[1]
        tall_flags = jnp.concatenate(
            [jnp.broadcast_to(slots[s : s + 1], (rows, lanes)) for s in range(groups * RS)], axis=0
        )
        shape = tall_flags.shape
        keep = within(iota(shape, 0), rows) == within(iota(shape, 1), rows)
        return jnp.where(keep, tall_flags, 0.0).astype(jnp.bfloat16)

    spot = jnp.where(valid_lanes[...] > 0, patch_lanes[...] * RS + row_lanes[...], -1)
    wide = count * blocks
    own_slots = same(iota((8, wide), 0) + me * RS == spot)
    own_slots = jnp.where(iota((8, wide), 0) < RS, own_slots, jnp.bfloat16(0))
    chunk = LANES // rows
    repeat = same(
        over(iota((chunk * blocks, LANES), 0), blocks) == over(iota((chunk * blocks, LANES), 1), rows)
    )
    own_flags = jnp.concatenate(
        [
            jnp.dot(
                own_slots[:, g * chunk * blocks : (g + 1) * chunk * blocks],
                repeat,
                preferred_element_type=jnp.float32,
            )
            for g in range(count // chunk)
        ],
        axis=1,
    )
    own_rows = spread(own_flags, 1)
    chosen[:patch_rows] = own_rows
    chosen[patch_rows:] = own_rows

    onehot = (iota((table_ref.shape[1], count), 0) == sets_lanes[...]).astype(jnp.float32)
    coeffs = jnp.dot(
        table_ref[...],
        onehot,
        precision=lax.Precision.HIGHEST,
        preferred_element_type=jnp.float32,
    )
    deep = count * rows
    coef_rows[...] = jnp.dot(
        coeffs,
        (iota((count, deep), 0) == over(iota((count, deep), 1), rows)).astype(jnp.float32),
        precision=lax.Precision.HIGHEST,
        preferred_element_type=jnp.float32,
    )

    shape = (planes * RS, wide)
    wanted = (mx * ny + over(iota(shape, 0), RS) * INNER + lo) * RS + within(iota(shape, 0), RS)
    shape = (wide, members * rows)
    member = over(iota(shape, 1), rows)
    exposure = over(member, INNER) * ny + hi * INNER + within(member, INNER)
    plane_flags = jnp.dot(
        same(wanted == spot),
        same(over(iota(shape, 0), blocks) == exposure),
        preferred_element_type=jnp.float32,
    )
    plane_rows = spread(plane_flags, planes)

    tap = iota((taps, LANES), 0)
    lane = iota((taps, LANES), 1)

    def laid(filters, where_to):
        return jnp.dot(
            filters,
            (lane == where_to).astype(jnp.float32),
            precision=lax.Precision.HIGHEST,
            preferred_element_type=jnp.float32,
        )

    across_pad[...] = laid(across_ref[...], tap)
    down_pad[...] = laid(down_ref[...], LANES - LEAD - tap)
    forward = iota((LANES, LANES), 1) >= iota((LANES, LANES), 0)
    first_half = iota((tall, LANES), 1) < patch_rows

    def build_bands(channel, carry):
        row = jnp.broadcast_to(across_pad[pl.ds(channel, 1), :], (LANES, LANES))
        band = pltpu.roll(row, 0, 1, stride=1, stride_axis=0)
        start_row = pl.multiple_of(channel * LANES, LANES)
        bands[pl.ds(start_row, LANES), :LANES] = jnp.where(forward, band, 0.0).astype(jnp.bfloat16)
        bands[pl.ds(start_row, LANES), LANES:] = jnp.where(forward, 0.0, band).astype(jnp.bfloat16)
        row = jnp.broadcast_to(down_pad[pl.ds(channel, 1), :], (tall, LANES))
        shifted = pltpu.roll(row, 0, 1, stride=1, stride_axis=0)
        high = shifted.astype(jnp.bfloat16).astype(jnp.float32)
        low = pltpu.roll(shifted - high, patch_rows, 1)
        start_row = pl.multiple_of(channel * tall, 16)
        shifts[pl.ds(start_row, tall), :] = jnp.where(first_half, high, low).astype(jnp.bfloat16)
        return carry

    lax.fori_loop(0, channels, build_bands, 0, unroll=4)

    def build_mixer(turn, carry):
        start_row = pl.multiple_of(turn * GROUP * tall, 16)
        picked = jnp.dot(
            shifts[pl.ds(start_row, GROUP * tall), :],
            chosen[...],
            preferred_element_type=jnp.float32,
        )
        for member in range(GROUP):
            mixed = picked[member * tall : (member + 1) * tall] * coef_rows[
                pl.ds(turn * GROUP + member, 1), :
            ]
            mixer[pl.ds(pl.multiple_of(start_row + member * tall, 16), tall), :] = mixed.astype(
                jnp.bfloat16
            )
        return carry

    lax.fori_loop(0, channels // GROUP, build_mixer, 0)

    def wait_keep(step, carry):
        tx, tlo = member_of(step)
        keep_copy(own_member, tx * INNER + tlo, (tx, hi * INNER + tlo)).wait_recv()
        return carry

    lax.fori_loop(1, members, wait_keep, 0)
    for plane in range(planes):
        part_send[plane % 2, plane // 2] = jnp.dot(
            plane_rows[plane * patch_rows : (plane + 1) * patch_rows],
            keep_recv[:, plane].reshape(members * rows, width),
            preferred_element_type=jnp.float32,
        ).astype(jnp.bfloat16)
    pair_copy().start()

    def wait_block(step, carry):
        tx, thi, tlo = partner(step)
        ty = thi * INNER + tlo
        block_copy(me, tx * ny + ty, (tx, ty)).wait_recv()
        return carry

    lax.fori_loop(0, count - 1, wait_block, 0)

    arrived = recv[...].reshape(deep, width)
    for turn in range(channels // GROUP):
        mixed = jnp.dot(
            mixer[turn * GROUP * tall : (turn + 1) * GROUP * tall],
            arrived,
            preferred_element_type=jnp.float32,
        ).astype(jnp.bfloat16)
        for member in range(GROUP):
            channel = turn * GROUP + member
            for t in range(tiles):
                mixed_tiles[
                    t * tall : (t + 1) * tall, channel * LANES : (channel + 1) * LANES
                ] = mixed[member * tall : (member + 1) * tall, t * LANES : (t + 1) * LANES]
    pair_copy().wait_recv()
    for place in range(half):
        merged[place] = (
            part_send[parity, place].astype(jnp.float32) + pair_recv[place].astype(jnp.float32)
        ).astype(jnp.bfloat16)
    part_recv[rank] = merged[rank]

    def rank_at(step):
        return lax.rem(rank + step, half)

    def device_at(place):
        return (mx, (place * 2 + parity) * INNER + lo)

    def start_part(step, carry):
        place = rank_at(step)
        part_copy(place, rank, device_at(place)).start()
        return carry

    lax.fori_loop(1, half, start_part, 0)
    summed = jnp.dot(mixed_tiles[...], bands[...], preferred_element_type=jnp.float32)
    zeros = jnp.zeros((tall, LANES), jnp.float32)
    now = [summed[t * tall : (t + 1) * tall, :LANES] for t in range(tiles)] + [zeros]
    after = [zeros] + [summed[t * tall : (t + 1) * tall, LANES:] for t in range(tiles)]
    joined = jnp.concatenate([a + b for a, b in zip(now, after)], axis=1)
    ext[...] = pltpu.roll(joined, width + LANES - margin, 1)

    top, middle, bottom = pl.ds(0, spill), pl.ds(spill, patch_rows), pl.ds(spill + patch_rows, spill)
    side, body_cols = pl.ds(width, LANES), pl.ds(0, width)
    plan = [
        (0, -1, (top, body_cols), edge_rows.at[1]),
        (0, 1, (bottom, body_cols), edge_rows.at[0]),
        (-1, 0, (middle, side), edge_cols.at[1]),
        (1, 0, (middle, side), edge_cols.at[0]),
        (-1, -1, (top, side), edge_corners.at[3]),
        (1, -1, (top, side), edge_corners.at[2]),
        (-1, 1, (bottom, side), edge_corners.at[1]),
        (1, 1, (bottom, side), edge_corners.at[0]),
    ]

    def exists(dx, dy):
        return (mx + dx >= 0) & (mx + dx < nx) & (my + dy >= 0) & (my + dy < ny)

    def edge_copy(number):
        dx, dy, piece, landing = plan[number]
        return pltpu.make_async_remote_copy(
            src_ref=ext.at[piece],
            dst_ref=landing,
            send_sem=edge_send_sem.at[number],
            recv_sem=edge_recv_sem.at[number],
            device_id=(mx + dx, my + dy),
            device_id_type=MESH,
        )

    for number, (dx, dy, _, _) in enumerate(plan):

        @pl.when(exists(dx, dy))
        def _():
            edge_copy(number).start()

    coadd_ref[...] = ext[middle, body_cols]

    def sent_block(step, carry):
        tx, thi, tlo = partner(step)
        ty = thi * INNER + tlo
        block_copy(tx * ny + ty, me, (tx, ty)).wait_send()
        return carry

    def sent_keep(step, carry):
        tx, tlo = member_of(step)
        keep_copy(tx * INNER + tlo, own_member, (tx, hi * INNER + tlo)).wait_send()
        return carry

    lax.fori_loop(0, count - 1, sent_block, 0)
    lax.fori_loop(1, members, sent_keep, 0)
    pair_copy().wait_send()
    lane = lax.broadcasted_iota(jnp.int32, (spill, LANES), 1)
    lane_tall = lax.broadcasted_iota(jnp.int32, (patch_rows, LANES), 1)
    low_rows, high_rows = pl.ds(0, spill), pl.ds(patch_rows - spill, spill)
    left, right = pl.ds(0, LANES), pl.ds(width - LANES, LANES)

    def from_side(value, lanes, dx):
        if dx < 0:
            return jnp.where(lanes < margin, value, 0.0)
        return jnp.where(lanes >= LANES - margin, value, 0.0)

    for number, (dx, dy, _, landing) in enumerate(plan):
        @pl.when(exists(-dx, -dy))
        def _():
            edge_copy(number).wait_recv()
            if dx == 0:
                here = low_rows if dy > 0 else high_rows
                coadd_ref[here, :] += landing[...]
            elif dy == 0:
                here = left if dx > 0 else right
                coadd_ref[:, here] += from_side(landing[...], lane_tall, -dx)
            else:
                here = (low_rows if dy > 0 else high_rows, left if dx > 0 else right)
                coadd_ref[here] += from_side(landing[...], lane, -dx)

    def sent_part(step, carry):
        place = rank_at(step)
        part_copy(place, rank, device_at(place)).wait_send()
        return carry

    def wait_part(step, carry):
        place = rank_at(step)
        part_copy(rank, place, device_at(place)).wait_recv()
        return carry

    lax.fori_loop(1, half, wait_part, 0)
    weights = part_recv[0].astype(jnp.float32)
    for place in range(1, half):
        weights = weights + part_recv[place].astype(jnp.float32)
    weight_ref[...] = weights

    lax.fori_loop(1, half, sent_part, 0)
    for number, (dx, dy, _, _) in enumerate(plan):

        @pl.when(exists(dx, dy))
        def _():
            edge_copy(number).wait_send()


def hand_out(coadd_ref, weight_ref, coadd_out, weight_out, sem):
    first = pltpu.make_async_copy(coadd_ref, coadd_out, sem.at[0])
    second = pltpu.make_async_copy(weight_ref, weight_out, sem.at[1])
    first.start()
    second.start()
    first.wait()
    second.wait()


def body(
    image, inverse_var, patch_of, row_of, valid, coef_index, coef_table, basis_across, basis_down
):
    nx, ny = lax.axis_size("skyx"), lax.axis_size("skyy")
    count = nx * ny
    planes, members = ny // INNER, nx * INNER
    blocks, rows, width = image.shape
    channels, taps = basis_across.shape
    margin = (taps - 1) // 2
    patch_rows = RS * rows
    spill = margin + LEAD
    tall = patch_rows + 2 * spill
    tiles = width // LANES
    deep = count * rows
    wide = count * blocks

    vmem = pl.BlockSpec(memory_space=pltpu.VMEM)
    operands = [
        image,
        inverse_var,
        patch_of.reshape(1, wide),
        row_of.reshape(1, wide),
        valid.reshape(1, wide),
        coef_index.reshape(1, count),
        coef_table.T,
        basis_across,
        basis_down,
    ]
    in_hbm = pl.BlockSpec(memory_space=pltpu.HBM)
    dma = pltpu.SemaphoreType.DMA
    outputs = pl.pallas_call(
        functools.partial(kernel, nx, ny, taps),
        out_shape=(
            jax.ShapeDtypeStruct((patch_rows, width), jnp.float32),
            jax.ShapeDtypeStruct((patch_rows, width), jnp.float32),
        ),
        in_specs=[in_hbm] * len(operands),
        out_specs=(vmem, vmem),
        scratch_shapes=[
            pltpu.VMEM((blocks, rows, width), jnp.bfloat16),
            pltpu.VMEM((blocks, rows, width), jnp.bfloat16),
            pltpu.SMEM((1, wide), jnp.int32),
            pltpu.SMEM((count,), jnp.int32),
            pltpu.VMEM((1, wide), jnp.int32),
            pltpu.VMEM((1, wide), jnp.int32),
            pltpu.VMEM((1, wide), jnp.int32),
            pltpu.VMEM((1, count), jnp.int32),
            pltpu.VMEM(coef_table.shape[::-1], jnp.float32),
            pltpu.VMEM((channels, taps), jnp.float32),
            pltpu.VMEM((channels, taps), jnp.float32),
            pltpu.VMEM((count, rows, width), jnp.bfloat16),
            pltpu.VMEM((count, rows, width), jnp.bfloat16),
            pltpu.VMEM((members, planes, rows, width), jnp.bfloat16),
            pltpu.VMEM((members, planes, rows, width), jnp.bfloat16),
            pltpu.VMEM((2, planes // 2, patch_rows, width), jnp.bfloat16),
            pltpu.VMEM((planes // 2, patch_rows, width), jnp.bfloat16),
            pltpu.VMEM((planes // 2, patch_rows, width), jnp.bfloat16),
            pltpu.VMEM((planes // 2, patch_rows, width), jnp.bfloat16),
            pltpu.VMEM((channels, LANES), jnp.float32),
            pltpu.VMEM((channels, LANES), jnp.float32),
            pltpu.VMEM((channels, deep), jnp.float32),
            pltpu.VMEM((2 * patch_rows, deep), jnp.bfloat16),
            pltpu.VMEM((channels * LANES, 2 * LANES), jnp.bfloat16),
            pltpu.VMEM((channels * tall, LANES), jnp.bfloat16),
            pltpu.VMEM((channels * tall, deep), jnp.bfloat16),
            pltpu.VMEM((tiles * tall, channels * LANES), jnp.bfloat16),
            pltpu.VMEM((tall, width + LANES), jnp.float32),
            pltpu.VMEM((2, spill, width), jnp.float32),
            pltpu.VMEM((2, patch_rows, LANES), jnp.float32),
            pltpu.VMEM((4, spill, LANES), jnp.float32),
            dma((10,)),
            dma((count,)),
            dma((count,)),
            dma((members,)),
            dma((members,)),
            dma((2,)),
            dma((planes // 2,)),
            dma((planes // 2,)),
            dma((8,)),
            dma((8,)),
        ],
        compiler_params=pltpu.CompilerParams(
            collective_id=0, has_side_effects=True, vmem_limit_bytes=(16 * 1024 + 256 * count) * 1024
        ),
    )(*[pltpu.with_memory_space_constraint(operand, pltpu.HBM) for operand in operands])
    return pl.pallas_call(
        hand_out,
        out_shape=tuple(jax.ShapeDtypeStruct(value.shape, value.dtype) for value in outputs),
        in_specs=[vmem, vmem],
        out_specs=(in_hbm, in_hbm),
        scratch_shapes=[dma((2,))],
    )(*outputs)


def solution(mesh):
    placed = (
        P(("skyx", "skyy"), None, None),
        P(("skyx", "skyy"), None, None),
        P(),
        P(),
        P(),
        P(),
        P(),
        P(),
        P(),
    )
    return jax.shard_map(
        body,
        mesh=mesh,
        in_specs=placed,
        out_specs=(P("skyy", "skyx"), P("skyy", "skyx")),
        check_vma=False,
    )
```

```python
import functools

import jax
import jax.numpy as jnp
from jax import lax
from jax.experimental import pallas as pl
from jax.experimental.pallas import tpu as pltpu
from jax.sharding import PartitionSpec as P

RS = 4
LANES = 128
LEAD = 4
INNER = 2
GROUP = 4
MESH = pl.DeviceIdType.MESH


def kernel(
    nx,
    ny,
    taps,
    image_hbm,
    ivar_hbm,
    patch_hbm,
    row_hbm,
    valid_hbm,
    sets_hbm,
    table_hbm,
    across_hbm,
    down_hbm,
    coadd_ref,
    weight_ref,
    image_ref,
    ivar_ref,
    patch_scalars,
    picks,
    patch_lanes,
    row_lanes,
    valid_lanes,
    sets_lanes,
    table_ref,
    across_ref,
    down_ref,
    send,
    recv,
    keep_send,
    keep_recv,
    part_send,
    pair_recv,
    merged,
    part_recv,
    across_pad,
    down_pad,
    coef_rows,
    chosen,
    bands,
    shifts,
    mixer,
    mixed_tiles,
    ext,
    edge_rows,
    edge_cols,
    edge_corners,
    load_sem,
    send_sem,
    recv_sem,
    keep_send_sem,
    keep_recv_sem,
    pair_sem,
    part_send_sem,
    part_recv_sem,
    edge_send_sem,
    edge_recv_sem,
):
    count = nx * ny
    planes = ny // INNER
    members = nx * INNER
    blocks, rows, width = image_ref.shape
    patch_rows = RS * rows
    channels = across_ref.shape[0]
    margin = (taps - 1) // 2
    tall = ext.shape[0]
    tiles = width // LANES
    spill = margin + LEAD
    mx = lax.axis_index("skyx")
    my = lax.axis_index("skyy")
    me = mx * ny + my
    hi, lo = my // INNER, lax.rem(my, INNER)

    def partner(step):
        back = count - 1 - step
        tx = lax.rem(mx + lax.rem(back // INNER, nx), nx)
        thi = lax.rem(hi + back // members, planes)
        tlo = lax.rem(lo + lax.rem(back, INNER), INNER)
        return tx, thi, tlo

    barrier = pltpu.get_barrier_semaphore()
    pairs = [
        (patch_hbm, patch_scalars),
        (image_hbm, image_ref),
        (ivar_hbm, ivar_ref),
        (patch_hbm, patch_lanes),
        (row_hbm, row_lanes),
        (valid_hbm, valid_lanes),
        (sets_hbm, sets_lanes),
        (table_hbm, table_ref),
        (across_hbm, across_ref),
        (down_hbm, down_ref),
    ]
    loads = [
        pltpu.make_async_copy(source, landing, load_sem.at[number])
        for number, (source, landing) in enumerate(pairs)
    ]
    for load in loads:
        load.start()

    def greet(step, carry):
        tx, thi, tlo = partner(step)
        pl.semaphore_signal(
            barrier, inc=1, device_id=(tx, thi * INNER + tlo), device_id_type=MESH
        )
        return carry

    lax.fori_loop(0, count - 1, greet, 0)
    loads[0].wait()
    targets = [patch_scalars[0, me * blocks + k] for k in range(blocks)]

    def find(patch, carry):
        block = 0
        for k in range(1, blocks):
            block = jnp.where(targets[k] == patch, k, block)
        picks[patch] = block
        return carry

    lax.fori_loop(0, count, find, 0)
    for load in loads[1:3]:
        load.wait()

    def stage(tx, thi, tlo):
        patch = tx * ny + thi * INNER + tlo
        block = picks[patch]
        weight = ivar_ref[block]
        product = weight.astype(jnp.float32) * image_ref[block].astype(jnp.float32)
        send[patch] = product.astype(jnp.bfloat16)
        keep_send[tx * INNER + tlo, thi] = weight

    def block_copy(target, source, device):
        return pltpu.make_async_remote_copy(
            src_ref=send.at[target],
            dst_ref=recv.at[source],
            send_sem=send_sem.at[target],
            recv_sem=recv_sem.at[source],
            device_id=device,
            device_id_type=MESH,
        )

    def keep_copy(target, source, device):
        return pltpu.make_async_remote_copy(
            src_ref=keep_send.at[target],
            dst_ref=keep_recv.at[source],
            send_sem=keep_send_sem.at[target],
            recv_sem=keep_recv_sem.at[source],
            device_id=device,
            device_id_type=MESH,
        )

    half = planes // 2
    parity, rank = lax.rem(hi, 2), hi // 2

    def pair_copy():
        return pltpu.make_async_remote_copy(
            src_ref=part_send.at[1 - parity],
            dst_ref=pair_recv,
            send_sem=pair_sem.at[0],
            recv_sem=pair_sem.at[1],
            device_id=(mx, (hi + 1 - 2 * parity) * INNER + lo),
            device_id_type=MESH,
        )

    def part_copy(target, source, device):
        return pltpu.make_async_remote_copy(
            src_ref=merged.at[target],
            dst_ref=part_recv.at[source],
            send_sem=part_send_sem.at[target],
            recv_sem=part_recv_sem.at[source],
            device_id=device,
            device_id_type=MESH,
        )

    def prepare(step, carry):
        stage(*partner(step))
        return carry

    lax.fori_loop(0, count, prepare, 0)
    pl.semaphore_wait(barrier, count - 1)

    def start(step, carry):
        tx, thi, tlo = partner(step)
        ty = thi * INNER + tlo
        block_copy(tx * ny + ty, me, (tx, ty)).start()
        return carry

    def member_of(step):
        return lax.rem(mx + step // INNER, nx), lax.rem(lo + lax.rem(step, INNER), INNER)

    own_member = mx * INNER + lo

    def start_keep(step, carry):
        tx, tlo = member_of(step)
        keep_copy(tx * INNER + tlo, own_member, (tx, hi * INNER + tlo)).start()
        return carry

    lax.fori_loop(1, members, start_keep, 0)
    lax.fori_loop(0, count - 1, start, 0)
    recv[me] = send[me]
    keep_recv[own_member] = keep_send[own_member]
    for load in loads[3:]:
        load.wait()

    def same(condition):
        return condition.astype(jnp.float32).astype(jnp.bfloat16)

    def iota(shape, dim):
        return lax.broadcasted_iota(jnp.int32, shape, dim)

    def over(value, by):
        return value >> (by.bit_length() - 1) if by & (by - 1) == 0 else value // by

    def within(value, by):
        return value & (by - 1) if by & (by - 1) == 0 else lax.rem(value, by)

    def spread(slots, groups):
        lanes = slots.shape[1]
        tall_flags = jnp.concatenate(
            [jnp.broadcast_to(slots[s : s + 1], (rows, lanes)) for s in range(groups * RS)], axis=0
        )
        shape = tall_flags.shape
        keep = within(iota(shape, 0), rows) == within(iota(shape, 1), rows)
        return jnp.where(keep, tall_flags, 0.0).astype(jnp.bfloat16)

    spot = jnp.where(valid_lanes[...] > 0, patch_lanes[...] * RS + row_lanes[...], -1)
    wide = count * blocks

    shape = (planes * RS, wide)
    wanted = (mx * ny + over(iota(shape, 0), RS) * INNER + lo) * RS + within(iota(shape, 0), RS)
    shape = (wide, members * rows)
    member = over(iota(shape, 1), rows)
    exposure = over(member, INNER) * ny + hi * INNER + within(member, INNER)
    plane_flags = jnp.dot(
        same(wanted == spot),
        same(over(iota(shape, 0), blocks) == exposure),
        preferred_element_type=jnp.float32,
    )
    plane_rows = spread(plane_flags, planes)

    def wait_keep(step, carry):
        tx, tlo = member_of(step)
        keep_copy(own_member, tx * INNER + tlo, (tx, hi * INNER + tlo)).wait_recv()
        return carry

    lax.fori_loop(1, members, wait_keep, 0)
    for plane in range(planes):
        part_send[plane % 2, plane // 2] = jnp.dot(
            plane_rows[plane * patch_rows : (plane + 1) * patch_rows],
            keep_recv[:, plane].reshape(members * rows, width),
            preferred_element_type=jnp.float32,
        ).astype(jnp.bfloat16)
    pair_copy().start()

    own_slots = same(iota((8, wide), 0) + me * RS == spot)
    own_slots = jnp.where(iota((8, wide), 0) < RS, own_slots, jnp.bfloat16(0))
    chunk = LANES // rows
    repeat = same(
        over(iota((chunk * blocks, LANES), 0), blocks) == over(iota((chunk * blocks, LANES), 1), rows)
    )
    own_flags = jnp.concatenate(
        [
            jnp.dot(
                own_slots[:, g * chunk * blocks : (g + 1) * chunk * blocks],
                repeat,
                preferred_element_type=jnp.float32,
            )
            for g in range(count // chunk)
        ],
        axis=1,
    )
    own_rows = spread(own_flags, 1)
    chosen[:patch_rows] = own_rows
    chosen[patch_rows:] = own_rows

    onehot = (iota((table_ref.shape[1], count), 0) == sets_lanes[...]).astype(jnp.float32)
    coeffs = jnp.dot(
        table_ref[...],
        onehot,
        precision=lax.Precision.HIGHEST,
        preferred_element_type=jnp.float32,
    )
    deep = count * rows
    coef_rows[...] = jnp.dot(
        coeffs,
        (iota((count, deep), 0) == over(iota((count, deep), 1), rows)).astype(jnp.float32),
        precision=lax.Precision.HIGHEST,
        preferred_element_type=jnp.float32,
    )

    tap = iota((taps, LANES), 0)
    lane = iota((taps, LANES), 1)

    def laid(filters, where_to):
        return jnp.dot(
            filters,
            (lane == where_to).astype(jnp.float32),
            precision=lax.Precision.HIGHEST,
            preferred_element_type=jnp.float32,
        )

    across_pad[...] = laid(across_ref[...], tap)
    down_pad[...] = laid(down_ref[...], LANES - LEAD - tap)
    forward = iota((LANES, LANES), 1) >= iota((LANES, LANES), 0)
    first_half = iota((tall, LANES), 1) < patch_rows

    def build_bands(channel, carry):
        row = jnp.broadcast_to(across_pad[pl.ds(channel, 1), :], (LANES, LANES))
        band = pltpu.roll(row, 0, 1, stride=1, stride_axis=0)
        start_row = pl.multiple_of(channel * LANES, LANES)
        bands[pl.ds(start_row, LANES), :LANES] = jnp.where(forward, band, 0.0).astype(jnp.bfloat16)
        bands[pl.ds(start_row, LANES), LANES:] = jnp.where(forward, 0.0, band).astype(jnp.bfloat16)
        row = jnp.broadcast_to(down_pad[pl.ds(channel, 1), :], (tall, LANES))
        shifted = pltpu.roll(row, 0, 1, stride=1, stride_axis=0)
        high = shifted.astype(jnp.bfloat16).astype(jnp.float32)
        low = pltpu.roll(shifted - high, patch_rows, 1)
        start_row = pl.multiple_of(channel * tall, 16)
        shifts[pl.ds(start_row, tall), :] = jnp.where(first_half, high, low).astype(jnp.bfloat16)
        return carry

    lax.fori_loop(0, channels, build_bands, 0, unroll=4)

    def build_mixer(turn, carry):
        start_row = pl.multiple_of(turn * GROUP * tall, 16)
        picked = jnp.dot(
            shifts[pl.ds(start_row, GROUP * tall), :],
            chosen[...],
            preferred_element_type=jnp.float32,
        )
        for member in range(GROUP):
            mixed = picked[member * tall : (member + 1) * tall] * coef_rows[
                pl.ds(turn * GROUP + member, 1), :
            ]
            mixer[pl.ds(pl.multiple_of(start_row + member * tall, 16), tall), :] = mixed.astype(
                jnp.bfloat16
            )
        return carry

    lax.fori_loop(0, channels // GROUP, build_mixer, 0)

    pair_copy().wait_recv()
    for place in range(half):
        merged[place] = (
            part_send[parity, place].astype(jnp.float32) + pair_recv[place].astype(jnp.float32)
        ).astype(jnp.bfloat16)
    part_recv[rank] = merged[rank]

    def rank_at(step):
        return lax.rem(rank + step, half)

    def device_at(place):
        return (mx, (place * 2 + parity) * INNER + lo)

    def start_part(step, carry):
        place = rank_at(step)
        part_copy(place, rank, device_at(place)).start()
        return carry

    lax.fori_loop(1, half, start_part, 0)

    def wait_block(step, carry):
        tx, thi, tlo = partner(step)
        ty = thi * INNER + tlo
        block_copy(me, tx * ny + ty, (tx, ty)).wait_recv()
        return carry

    lax.fori_loop(0, count - 1, wait_block, 0)

    arrived = recv[...].reshape(deep, width)
    for turn in range(channels // GROUP):
        mixed = jnp.dot(
            mixer[turn * GROUP * tall : (turn + 1) * GROUP * tall],
            arrived,
            preferred_element_type=jnp.float32,
        ).astype(jnp.bfloat16)
        for member in range(GROUP):
            channel = turn * GROUP + member
            for t in range(tiles):
                mixed_tiles[
                    t * tall : (t + 1) * tall, channel * LANES : (channel + 1) * LANES
                ] = mixed[member * tall : (member + 1) * tall, t * LANES : (t + 1) * LANES]
    summed = jnp.dot(mixed_tiles[...], bands[...], preferred_element_type=jnp.float32)
    zeros = jnp.zeros((tall, LANES), jnp.float32)
    now = [summed[t * tall : (t + 1) * tall, :LANES] for t in range(tiles)] + [zeros]
    after = [zeros] + [summed[t * tall : (t + 1) * tall, LANES:] for t in range(tiles)]
    joined = jnp.concatenate([a + b for a, b in zip(now, after)], axis=1)
    ext[...] = pltpu.roll(joined, width + LANES - margin, 1)

    top, middle, bottom = pl.ds(0, spill), pl.ds(spill, patch_rows), pl.ds(spill + patch_rows, spill)
    side, body_cols = pl.ds(width, LANES), pl.ds(0, width)
    plan = [
        (0, -1, (top, body_cols), edge_rows.at[1]),
        (0, 1, (bottom, body_cols), edge_rows.at[0]),
        (-1, 0, (middle, side), edge_cols.at[1]),
        (1, 0, (middle, side), edge_cols.at[0]),
        (-1, -1, (top, side), edge_corners.at[3]),
        (1, -1, (top, side), edge_corners.at[2]),
        (-1, 1, (bottom, side), edge_corners.at[1]),
        (1, 1, (bottom, side), edge_corners.at[0]),
    ]

    def exists(dx, dy):
        return (mx + dx >= 0) & (mx + dx < nx) & (my + dy >= 0) & (my + dy < ny)

    def edge_copy(number):
        dx, dy, piece, landing = plan[number]
        return pltpu.make_async_remote_copy(
            src_ref=ext.at[piece],
            dst_ref=landing,
            send_sem=edge_send_sem.at[number],
            recv_sem=edge_recv_sem.at[number],
            device_id=(mx + dx, my + dy),
            device_id_type=MESH,
        )

    for number, (dx, dy, _, _) in enumerate(plan):

        @pl.when(exists(dx, dy))
        def _():
            edge_copy(number).start()

    coadd_ref[...] = ext[middle, body_cols]

    def sent_block(step, carry):
        tx, thi, tlo = partner(step)
        ty = thi * INNER + tlo
        block_copy(tx * ny + ty, me, (tx, ty)).wait_send()
        return carry

    def sent_keep(step, carry):
        tx, tlo = member_of(step)
        keep_copy(tx * INNER + tlo, own_member, (tx, hi * INNER + tlo)).wait_send()
        return carry

    lax.fori_loop(0, count - 1, sent_block, 0)
    lax.fori_loop(1, members, sent_keep, 0)
    pair_copy().wait_send()
    lane = lax.broadcasted_iota(jnp.int32, (spill, LANES), 1)
    lane_tall = lax.broadcasted_iota(jnp.int32, (patch_rows, LANES), 1)
    low_rows, high_rows = pl.ds(0, spill), pl.ds(patch_rows - spill, spill)
    left, right = pl.ds(0, LANES), pl.ds(width - LANES, LANES)

    def from_side(value, lanes, dx):
        if dx < 0:
            return jnp.where(lanes < margin, value, 0.0)
        return jnp.where(lanes >= LANES - margin, value, 0.0)

    for number, (dx, dy, _, landing) in enumerate(plan):
        @pl.when(exists(-dx, -dy))
        def _():
            edge_copy(number).wait_recv()
            if dx == 0:
                here = low_rows if dy > 0 else high_rows
                coadd_ref[here, :] += landing[...]
            elif dy == 0:
                here = left if dx > 0 else right
                coadd_ref[:, here] += from_side(landing[...], lane_tall, -dx)
            else:
                here = (low_rows if dy > 0 else high_rows, left if dx > 0 else right)
                coadd_ref[here] += from_side(landing[...], lane, -dx)

    def sent_part(step, carry):
        place = rank_at(step)
        part_copy(place, rank, device_at(place)).wait_send()
        return carry

    def wait_part(step, carry):
        place = rank_at(step)
        part_copy(rank, place, device_at(place)).wait_recv()
        return carry

    lax.fori_loop(1, half, wait_part, 0)
    weights = part_recv[0].astype(jnp.float32)
    for place in range(1, half):
        weights = weights + part_recv[place].astype(jnp.float32)
    weight_ref[...] = weights

    lax.fori_loop(1, half, sent_part, 0)
    for number, (dx, dy, _, _) in enumerate(plan):

        @pl.when(exists(dx, dy))
        def _():
            edge_copy(number).wait_send()


def body(
    image, inverse_var, patch_of, row_of, valid, coef_index, coef_table, basis_across, basis_down
):
    nx, ny = lax.axis_size("skyx"), lax.axis_size("skyy")
    count = nx * ny
    planes, members = ny // INNER, nx * INNER
    blocks, rows, width = image.shape
    channels, taps = basis_across.shape
    margin = (taps - 1) // 2
    patch_rows = RS * rows
    spill = margin + LEAD
    tall = patch_rows + 2 * spill
    tiles = width // LANES
    deep = count * rows
    wide = count * blocks

    vmem = pl.BlockSpec(memory_space=pltpu.VMEM)
    operands = [
        image,
        inverse_var,
        patch_of.reshape(1, wide),
        row_of.reshape(1, wide),
        valid.reshape(1, wide),
        coef_index.reshape(1, count),
        coef_table.T,
        basis_across,
        basis_down,
    ]
    in_hbm = pl.BlockSpec(memory_space=pltpu.HBM)
    dma = pltpu.SemaphoreType.DMA
    return pl.pallas_call(
        functools.partial(kernel, nx, ny, taps),
        out_shape=(
            jax.ShapeDtypeStruct((patch_rows, width), jnp.float32),
            jax.ShapeDtypeStruct((patch_rows, width), jnp.float32),
        ),
        in_specs=[in_hbm] * len(operands),
        out_specs=(vmem, vmem),
        scratch_shapes=[
            pltpu.VMEM((blocks, rows, width), jnp.bfloat16),
            pltpu.VMEM((blocks, rows, width), jnp.bfloat16),
            pltpu.SMEM((1, wide), jnp.int32),
            pltpu.SMEM((count,), jnp.int32),
            pltpu.VMEM((1, wide), jnp.int32),
            pltpu.VMEM((1, wide), jnp.int32),
            pltpu.VMEM((1, wide), jnp.int32),
            pltpu.VMEM((1, count), jnp.int32),
            pltpu.VMEM(coef_table.shape[::-1], jnp.float32),
            pltpu.VMEM((channels, taps), jnp.float32),
            pltpu.VMEM((channels, taps), jnp.float32),
            pltpu.VMEM((count, rows, width), jnp.bfloat16),
            pltpu.VMEM((count, rows, width), jnp.bfloat16),
            pltpu.VMEM((members, planes, rows, width), jnp.bfloat16),
            pltpu.VMEM((members, planes, rows, width), jnp.bfloat16),
            pltpu.VMEM((2, planes // 2, patch_rows, width), jnp.bfloat16),
            pltpu.VMEM((planes // 2, patch_rows, width), jnp.bfloat16),
            pltpu.VMEM((planes // 2, patch_rows, width), jnp.bfloat16),
            pltpu.VMEM((planes // 2, patch_rows, width), jnp.bfloat16),
            pltpu.VMEM((channels, LANES), jnp.float32),
            pltpu.VMEM((channels, LANES), jnp.float32),
            pltpu.VMEM((channels, deep), jnp.float32),
            pltpu.VMEM((2 * patch_rows, deep), jnp.bfloat16),
            pltpu.VMEM((channels * LANES, 2 * LANES), jnp.bfloat16),
            pltpu.VMEM((channels * tall, LANES), jnp.bfloat16),
            pltpu.VMEM((channels * tall, deep), jnp.bfloat16),
            pltpu.VMEM((tiles * tall, channels * LANES), jnp.bfloat16),
            pltpu.VMEM((tall, width + LANES), jnp.float32),
            pltpu.VMEM((2, spill, width), jnp.float32),
            pltpu.VMEM((2, patch_rows, LANES), jnp.float32),
            pltpu.VMEM((4, spill, LANES), jnp.float32),
            dma((10,)),
            dma((count,)),
            dma((count,)),
            dma((members,)),
            dma((members,)),
            dma((2,)),
            dma((planes // 2,)),
            dma((planes // 2,)),
            dma((8,)),
            dma((8,)),
        ],
        compiler_params=pltpu.CompilerParams(
            collective_id=0, has_side_effects=True, vmem_limit_bytes=(16 * 1024 + 256 * count) * 1024
        ),
    )(*[pltpu.with_memory_space_constraint(operand, pltpu.HBM) for operand in operands])


def solution(mesh):
    placed = (
        P(("skyx", "skyy"), None, None),
        P(("skyx", "skyy"), None, None),
        P(),
        P(),
        P(),
        P(),
        P(),
        P(),
        P(),
    )
    return jax.shard_map(
        body,
        mesh=mesh,
        in_specs=placed,
        out_specs=(P("skyy", "skyx"), P("skyy", "skyx")),
        check_vma=False,
    )
```

```python
import functools

import jax
import jax.numpy as jnp
from jax import lax
from jax.experimental import pallas as pl
from jax.experimental.pallas import tpu as pltpu
from jax.sharding import PartitionSpec as P

RS = 4
LANES = 128
LEAD = 4
INNER = 2
GROUP = 4
MESH = pl.DeviceIdType.MESH


def kernel(
    nx,
    ny,
    taps,
    image_hbm,
    ivar_hbm,
    patch_hbm,
    row_hbm,
    valid_hbm,
    sets_hbm,
    table_hbm,
    across_hbm,
    down_hbm,
    coadd_ref,
    weight_ref,
    image_ref,
    ivar_ref,
    patch_scalars,
    picks,
    patch_lanes,
    row_lanes,
    valid_lanes,
    sets_lanes,
    table_ref,
    across_ref,
    down_ref,
    send,
    recv,
    keep_send,
    keep_recv,
    part_send,
    pair_recv,
    merged,
    part_recv,
    across_pad,
    down_pad,
    coef_rows,
    chosen,
    bands,
    shifts,
    mixer,
    mixed_tiles,
    ext,
    edge_rows,
    edge_cols,
    edge_corners,
    load_sem,
    send_sem,
    recv_sem,
    keep_send_sem,
    keep_recv_sem,
    pair_sem,
    part_send_sem,
    part_recv_sem,
    edge_send_sem,
    edge_recv_sem,
):
    count = nx * ny
    planes = ny // INNER
    members = nx * INNER
    blocks, rows, width = image_ref.shape
    patch_rows = RS * rows
    channels = across_ref.shape[0]
    margin = (taps - 1) // 2
    tall = ext.shape[0]
    tiles = width // LANES
    spill = margin + LEAD
    mx = lax.axis_index("skyx")
    my = lax.axis_index("skyy")
    me = mx * ny + my
    hi, lo = my // INNER, lax.rem(my, INNER)

    def plane_across(distance):
        if planes & (planes - 1):
            return lax.rem(hi + distance, planes)
        plane = 0
        for bit in range(planes.bit_length() - 1):
            power = 1 << bit
            plane = plane + lax.rem(hi // power + distance // power, 2) * power
        return plane

    def partner(step):
        back = count - 1 - step
        tx = lax.rem(mx + lax.rem(back // INNER, nx), nx)
        thi = plane_across(back // members)
        tlo = lax.rem(lo + lax.rem(back, INNER), INNER)
        return tx, thi, tlo

    barrier = pltpu.get_barrier_semaphore()
    pairs = [
        (patch_hbm, patch_scalars),
        (image_hbm, image_ref),
        (ivar_hbm, ivar_ref),
        (patch_hbm, patch_lanes),
        (row_hbm, row_lanes),
        (valid_hbm, valid_lanes),
        (sets_hbm, sets_lanes),
        (table_hbm, table_ref),
        (across_hbm, across_ref),
        (down_hbm, down_ref),
    ]
    loads = [
        pltpu.make_async_copy(source, landing, load_sem.at[number])
        for number, (source, landing) in enumerate(pairs)
    ]
    for load in loads:
        load.start()

    def greet(step, carry):
        tx, thi, tlo = partner(step)
        pl.semaphore_signal(
            barrier, inc=1, device_id=(tx, thi * INNER + tlo), device_id_type=MESH
        )
        return carry

    lax.fori_loop(0, count - 1, greet, 0)
    loads[0].wait()
    targets = [patch_scalars[0, me * blocks + k] for k in range(blocks)]

    def find(patch, carry):
        block = 0
        for k in range(1, blocks):
            block = jnp.where(targets[k] == patch, k, block)
        picks[patch] = block
        return carry

    lax.fori_loop(0, count, find, 0)
    for load in loads[1:3]:
        load.wait()

    def stage(tx, thi, tlo):
        patch = tx * ny + thi * INNER + tlo
        block = picks[patch]
        weight = ivar_ref[block]
        product = weight.astype(jnp.float32) * image_ref[block].astype(jnp.float32)
        send[patch] = product.astype(jnp.bfloat16)
        keep_send[tx * INNER + tlo, thi] = weight

    def block_copy(target, source, device):
        return pltpu.make_async_remote_copy(
            src_ref=send.at[target],
            dst_ref=recv.at[source],
            send_sem=send_sem.at[target],
            recv_sem=recv_sem.at[source],
            device_id=device,
            device_id_type=MESH,
        )

    def keep_copy(target, source, device):
        return pltpu.make_async_remote_copy(
            src_ref=keep_send.at[target],
            dst_ref=keep_recv.at[source],
            send_sem=keep_send_sem.at[target],
            recv_sem=keep_recv_sem.at[source],
            device_id=device,
            device_id_type=MESH,
        )

    half = planes // 2
    parity, rank = lax.rem(hi, 2), hi // 2

    def pair_copy():
        return pltpu.make_async_remote_copy(
            src_ref=part_send.at[1 - parity],
            dst_ref=pair_recv,
            send_sem=pair_sem.at[0],
            recv_sem=pair_sem.at[1],
            device_id=(mx, (hi + 1 - 2 * parity) * INNER + lo),
            device_id_type=MESH,
        )

    def part_copy(target, source, device):
        return pltpu.make_async_remote_copy(
            src_ref=merged.at[target],
            dst_ref=part_recv.at[source],
            send_sem=part_send_sem.at[target],
            recv_sem=part_recv_sem.at[source],
            device_id=device,
            device_id_type=MESH,
        )

    def prepare(step, carry):
        stage(*partner(step))
        return carry

    lax.fori_loop(0, count, prepare, 0)
    pl.semaphore_wait(barrier, count - 1)

    def start(step, carry):
        tx, thi, tlo = partner(step)
        ty = thi * INNER + tlo
        block_copy(tx * ny + ty, me, (tx, ty)).start()
        return carry

    lax.fori_loop(0, count - members, start, 0)

    def member_of(step):
        return lax.rem(mx + step // INNER, nx), lax.rem(lo + lax.rem(step, INNER), INNER)

    own_member = mx * INNER + lo

    def start_keep(step, carry):
        tx, tlo = member_of(step)
        keep_copy(tx * INNER + tlo, own_member, (tx, hi * INNER + tlo)).start()
        return carry

    lax.fori_loop(1, members, start_keep, 0)
    lax.fori_loop(count - members, count - 1, start, 0)
    recv[me] = send[me]
    keep_recv[own_member] = keep_send[own_member]
    for load in loads[3:]:
        load.wait()

    def same(condition):
        return condition.astype(jnp.float32).astype(jnp.bfloat16)

    def iota(shape, dim):
        return lax.broadcasted_iota(jnp.int32, shape, dim)

    def over(value, by):
        return value >> (by.bit_length() - 1) if by & (by - 1) == 0 else value // by

    def within(value, by):
        return value & (by - 1) if by & (by - 1) == 0 else lax.rem(value, by)

    def spread(slots, groups):
        lanes = slots.shape[1]
        tall_flags = jnp.concatenate(
            [jnp.broadcast_to(slots[s : s + 1], (rows, lanes)) for s in range(groups * RS)], axis=0
        )
        shape = tall_flags.shape
        keep = within(iota(shape, 0), rows) == within(iota(shape, 1), rows)
        return jnp.where(keep, tall_flags, 0.0).astype(jnp.bfloat16)

    spot = jnp.where(valid_lanes[...] > 0, patch_lanes[...] * RS + row_lanes[...], -1)
    wide = count * blocks
    own_slots = same(iota((8, wide), 0) + me * RS == spot)
    own_slots = jnp.where(iota((8, wide), 0) < RS, own_slots, jnp.bfloat16(0))
    chunk = LANES // rows
    repeat = same(
        over(iota((chunk * blocks, LANES), 0), blocks) == over(iota((chunk * blocks, LANES), 1), rows)
    )
    own_flags = jnp.concatenate(
        [
            jnp.dot(
                own_slots[:, g * chunk * blocks : (g + 1) * chunk * blocks],
                repeat,
                preferred_element_type=jnp.float32,
            )
            for g in range(count // chunk)
        ],
        axis=1,
    )
    own_rows = spread(own_flags, 1)
    chosen[:patch_rows] = own_rows
    chosen[patch_rows:] = own_rows

    onehot = (iota((table_ref.shape[1], count), 0) == sets_lanes[...]).astype(jnp.float32)
    coeffs = jnp.dot(
        table_ref[...],
        onehot,
        precision=lax.Precision.HIGHEST,
        preferred_element_type=jnp.float32,
    )
    deep = count * rows
    coef_rows[...] = jnp.dot(
        coeffs,
        (iota((count, deep), 0) == over(iota((count, deep), 1), rows)).astype(jnp.float32),
        precision=lax.Precision.HIGHEST,
        preferred_element_type=jnp.float32,
    )

    shape = (planes * RS, wide)
    wanted = (mx * ny + over(iota(shape, 0), RS) * INNER + lo) * RS + within(iota(shape, 0), RS)
    shape = (wide, members * rows)
    member = over(iota(shape, 1), rows)
    exposure = over(member, INNER) * ny + hi * INNER + within(member, INNER)
    plane_flags = jnp.dot(
        same(wanted == spot),
        same(over(iota(shape, 0), blocks) == exposure),
        preferred_element_type=jnp.float32,
    )
    plane_rows = spread(plane_flags, planes)

    tap = iota((taps, LANES), 0)
    lane = iota((taps, LANES), 1)

    def laid(filters, where_to):
        return jnp.dot(
            filters,
            (lane == where_to).astype(jnp.float32),
            precision=lax.Precision.HIGHEST,
            preferred_element_type=jnp.float32,
        )

    across_pad[...] = laid(across_ref[...], tap)
    down_pad[...] = laid(down_ref[...], LANES - LEAD - tap)
    forward = iota((LANES, LANES), 1) >= iota((LANES, LANES), 0)
    first_half = iota((tall, LANES), 1) < patch_rows

    def build_bands(channel, carry):
        row = jnp.broadcast_to(across_pad[pl.ds(channel, 1), :], (LANES, LANES))
        band = pltpu.roll(row, 0, 1, stride=1, stride_axis=0)
        start_row = pl.multiple_of(channel * LANES, LANES)
        bands[pl.ds(start_row, LANES), :LANES] = jnp.where(forward, band, 0.0).astype(jnp.bfloat16)
        bands[pl.ds(start_row, LANES), LANES:] = jnp.where(forward, 0.0, band).astype(jnp.bfloat16)
        row = jnp.broadcast_to(down_pad[pl.ds(channel, 1), :], (tall, LANES))
        shifted = pltpu.roll(row, 0, 1, stride=1, stride_axis=0)
        high = shifted.astype(jnp.bfloat16).astype(jnp.float32)
        low = pltpu.roll(shifted - high, patch_rows, 1)
        start_row = pl.multiple_of(channel * tall, 16)
        shifts[pl.ds(start_row, tall), :] = jnp.where(first_half, high, low).astype(jnp.bfloat16)
        return carry

    lax.fori_loop(0, channels, build_bands, 0, unroll=4)

    def build_mixer(turn, carry):
        start_row = pl.multiple_of(turn * GROUP * tall, 16)
        picked = jnp.dot(
            shifts[pl.ds(start_row, GROUP * tall), :],
            chosen[...],
            preferred_element_type=jnp.float32,
        )
        for member in range(GROUP):
            mixed = picked[member * tall : (member + 1) * tall] * coef_rows[
                pl.ds(turn * GROUP + member, 1), :
            ]
            mixer[pl.ds(pl.multiple_of(start_row + member * tall, 16), tall), :] = mixed.astype(
                jnp.bfloat16
            )
        return carry

    lax.fori_loop(0, channels // GROUP, build_mixer, 0)

    def wait_keep(step, carry):
        tx, tlo = member_of(step)
        keep_copy(own_member, tx * INNER + tlo, (tx, hi * INNER + tlo)).wait_recv()
        return carry

    lax.fori_loop(1, members, wait_keep, 0)
    for plane in range(planes):
        part_send[plane % 2, plane // 2] = jnp.dot(
            plane_rows[plane * patch_rows : (plane + 1) * patch_rows],
            keep_recv[:, plane].reshape(members * rows, width),
            preferred_element_type=jnp.float32,
        ).astype(jnp.bfloat16)
    pair_copy().start()

    def wait_block(step, carry):
        tx, thi, tlo = partner(step)
        ty = thi * INNER + tlo
        block_copy(me, tx * ny + ty, (tx, ty)).wait_recv()
        return carry

    lax.fori_loop(0, count - 1, wait_block, 0)

    arrived = recv[...].reshape(deep, width)
    for turn in range(channels // GROUP):
        mixed = jnp.dot(
            mixer[turn * GROUP * tall : (turn + 1) * GROUP * tall],
            arrived,
            preferred_element_type=jnp.float32,
        ).astype(jnp.bfloat16)
        for member in range(GROUP):
            channel = turn * GROUP + member
            for t in range(tiles):
                mixed_tiles[
                    t * tall : (t + 1) * tall, channel * LANES : (channel + 1) * LANES
                ] = mixed[member * tall : (member + 1) * tall, t * LANES : (t + 1) * LANES]
    summed = jnp.dot(mixed_tiles[...], bands[...], preferred_element_type=jnp.float32)
    zeros = jnp.zeros((tall, LANES), jnp.float32)
    now = [summed[t * tall : (t + 1) * tall, :LANES] for t in range(tiles)] + [zeros]
    after = [zeros] + [summed[t * tall : (t + 1) * tall, LANES:] for t in range(tiles)]
    joined = jnp.concatenate([a + b for a, b in zip(now, after)], axis=1)
    ext[...] = pltpu.roll(joined, width + LANES - margin, 1)

    top, middle, bottom = pl.ds(0, spill), pl.ds(spill, patch_rows), pl.ds(spill + patch_rows, spill)
    side, body_cols = pl.ds(width, LANES), pl.ds(0, width)
    plan = [
        (0, -1, (top, body_cols), edge_rows.at[1]),
        (0, 1, (bottom, body_cols), edge_rows.at[0]),
        (-1, 0, (middle, side), edge_cols.at[1]),
        (1, 0, (middle, side), edge_cols.at[0]),
        (-1, -1, (top, side), edge_corners.at[3]),
        (1, -1, (top, side), edge_corners.at[2]),
        (-1, 1, (bottom, side), edge_corners.at[1]),
        (1, 1, (bottom, side), edge_corners.at[0]),
    ]

    def exists(dx, dy):
        return (mx + dx >= 0) & (mx + dx < nx) & (my + dy >= 0) & (my + dy < ny)

    def edge_copy(number):
        dx, dy, piece, landing = plan[number]
        return pltpu.make_async_remote_copy(
            src_ref=ext.at[piece],
            dst_ref=landing,
            send_sem=edge_send_sem.at[number],
            recv_sem=edge_recv_sem.at[number],
            device_id=(mx + dx, my + dy),
            device_id_type=MESH,
        )

    for number, (dx, dy, _, _) in enumerate(plan):

        @pl.when(exists(dx, dy))
        def _():
            edge_copy(number).start()

    coadd_ref[...] = ext[middle, body_cols]

    pair_copy().wait_recv()
    for place in range(half):
        merged[place] = (
            part_send[parity, place].astype(jnp.float32) + pair_recv[place].astype(jnp.float32)
        ).astype(jnp.bfloat16)
    part_recv[rank] = merged[rank]

    def rank_at(step):
        return lax.rem(rank + step, half)

    def device_at(place):
        return (mx, (place * 2 + parity) * INNER + lo)

    def start_part(step, carry):
        place = rank_at(step)
        part_copy(place, rank, device_at(place)).start()
        return carry

    lax.fori_loop(1, half, start_part, 0)
    def sent_block(step, carry):
        tx, thi, tlo = partner(step)
        ty = thi * INNER + tlo
        block_copy(tx * ny + ty, me, (tx, ty)).wait_send()
        return carry

    def sent_keep(step, carry):
        tx, tlo = member_of(step)
        keep_copy(tx * INNER + tlo, own_member, (tx, hi * INNER + tlo)).wait_send()
        return carry

    lax.fori_loop(0, count - 1, sent_block, 0)
    lax.fori_loop(1, members, sent_keep, 0)
    pair_copy().wait_send()
    lane = lax.broadcasted_iota(jnp.int32, (spill, LANES), 1)
    lane_tall = lax.broadcasted_iota(jnp.int32, (patch_rows, LANES), 1)
    low_rows, high_rows = pl.ds(0, spill), pl.ds(patch_rows - spill, spill)
    left, right = pl.ds(0, LANES), pl.ds(width - LANES, LANES)

    def from_side(value, lanes, dx):
        if dx < 0:
            return jnp.where(lanes < margin, value, 0.0)
        return jnp.where(lanes >= LANES - margin, value, 0.0)

    for number, (dx, dy, _, landing) in enumerate(plan):
        @pl.when(exists(-dx, -dy))
        def _():
            edge_copy(number).wait_recv()
            if dx == 0:
                here = low_rows if dy > 0 else high_rows
                coadd_ref[here, :] += landing[...]
            elif dy == 0:
                here = left if dx > 0 else right
                coadd_ref[:, here] += from_side(landing[...], lane_tall, -dx)
            else:
                here = (low_rows if dy > 0 else high_rows, left if dx > 0 else right)
                coadd_ref[here] += from_side(landing[...], lane, -dx)

    def sent_part(step, carry):
        place = rank_at(step)
        part_copy(place, rank, device_at(place)).wait_send()
        return carry

    def wait_part(step, carry):
        place = rank_at(step)
        part_copy(rank, place, device_at(place)).wait_recv()
        return carry

    lax.fori_loop(1, half, wait_part, 0)
    weights = part_recv[0].astype(jnp.float32)
    for place in range(1, half):
        weights = weights + part_recv[place].astype(jnp.float32)
    weight_ref[...] = weights

    lax.fori_loop(1, half, sent_part, 0)
    for number, (dx, dy, _, _) in enumerate(plan):

        @pl.when(exists(dx, dy))
        def _():
            edge_copy(number).wait_send()


def body(
    image, inverse_var, patch_of, row_of, valid, coef_index, coef_table, basis_across, basis_down
):
    nx, ny = lax.axis_size("skyx"), lax.axis_size("skyy")
    count = nx * ny
    planes, members = ny // INNER, nx * INNER
    blocks, rows, width = image.shape
    channels, taps = basis_across.shape
    margin = (taps - 1) // 2
    patch_rows = RS * rows
    spill = margin + LEAD
    tall = patch_rows + 2 * spill
    tiles = width // LANES
    deep = count * rows
    wide = count * blocks

    vmem = pl.BlockSpec(memory_space=pltpu.VMEM)
    operands = [
        image,
        inverse_var,
        patch_of.reshape(1, wide),
        row_of.reshape(1, wide),
        valid.reshape(1, wide),
        coef_index.reshape(1, count),
        coef_table.T,
        basis_across,
        basis_down,
    ]
    in_hbm = pl.BlockSpec(memory_space=pltpu.HBM)
    dma = pltpu.SemaphoreType.DMA
    return pl.pallas_call(
        functools.partial(kernel, nx, ny, taps),
        out_shape=(
            jax.ShapeDtypeStruct((patch_rows, width), jnp.float32),
            jax.ShapeDtypeStruct((patch_rows, width), jnp.float32),
        ),
        in_specs=[in_hbm] * len(operands),
        out_specs=(vmem, vmem),
        scratch_shapes=[
            pltpu.VMEM((blocks, rows, width), jnp.bfloat16),
            pltpu.VMEM((blocks, rows, width), jnp.bfloat16),
            pltpu.SMEM((1, wide), jnp.int32),
            pltpu.SMEM((count,), jnp.int32),
            pltpu.VMEM((1, wide), jnp.int32),
            pltpu.VMEM((1, wide), jnp.int32),
            pltpu.VMEM((1, wide), jnp.int32),
            pltpu.VMEM((1, count), jnp.int32),
            pltpu.VMEM(coef_table.shape[::-1], jnp.float32),
            pltpu.VMEM((channels, taps), jnp.float32),
            pltpu.VMEM((channels, taps), jnp.float32),
            pltpu.VMEM((count, rows, width), jnp.bfloat16),
            pltpu.VMEM((count, rows, width), jnp.bfloat16),
            pltpu.VMEM((members, planes, rows, width), jnp.bfloat16),
            pltpu.VMEM((members, planes, rows, width), jnp.bfloat16),
            pltpu.VMEM((2, planes // 2, patch_rows, width), jnp.bfloat16),
            pltpu.VMEM((planes // 2, patch_rows, width), jnp.bfloat16),
            pltpu.VMEM((planes // 2, patch_rows, width), jnp.bfloat16),
            pltpu.VMEM((planes // 2, patch_rows, width), jnp.bfloat16),
            pltpu.VMEM((channels, LANES), jnp.float32),
            pltpu.VMEM((channels, LANES), jnp.float32),
            pltpu.VMEM((channels, deep), jnp.float32),
            pltpu.VMEM((2 * patch_rows, deep), jnp.bfloat16),
            pltpu.VMEM((channels * LANES, 2 * LANES), jnp.bfloat16),
            pltpu.VMEM((channels * tall, LANES), jnp.bfloat16),
            pltpu.VMEM((channels * tall, deep), jnp.bfloat16),
            pltpu.VMEM((tiles * tall, channels * LANES), jnp.bfloat16),
            pltpu.VMEM((tall, width + LANES), jnp.float32),
            pltpu.VMEM((2, spill, width), jnp.float32),
            pltpu.VMEM((2, patch_rows, LANES), jnp.float32),
            pltpu.VMEM((4, spill, LANES), jnp.float32),
            dma((10,)),
            dma((count,)),
            dma((count,)),
            dma((members,)),
            dma((members,)),
            dma((2,)),
            dma((planes // 2,)),
            dma((planes // 2,)),
            dma((8,)),
            dma((8,)),
        ],
        compiler_params=pltpu.CompilerParams(
            collective_id=0, has_side_effects=True, vmem_limit_bytes=(16 * 1024 + 256 * count) * 1024
        ),
    )(*[pltpu.with_memory_space_constraint(operand, pltpu.HBM) for operand in operands])


def solution(mesh):
    placed = (
        P(("skyx", "skyy"), None, None),
        P(("skyx", "skyy"), None, None),
        P(),
        P(),
        P(),
        P(),
        P(),
        P(),
        P(),
    )
    return jax.shard_map(
        body,
        mesh=mesh,
        in_specs=placed,
        out_specs=(P("skyy", "skyx"), P("skyy", "skyx")),
        check_vma=False,
    )
```
